256 devices in a mesh: env: 8 (over y_hi, x), sp: 32 (over z, y_lo, core).
Axes of the slice: x: 4, y: 4 (y_hi: 2, y_lo: 2; y = y_hi * 2 + y_lo), z: 8, core: 2. Of those that a mesh axis runs over, the one named last changes fastest.
Arguments:
- descriptors: bfloat16 [16384, 512], P('env'), may hold values from -6 to 6
- sparse_points: bfloat16 [8192, 512], P('sp'), may hold values from -6 to 6
Outputs:
- gram_bands: float32 [32, 17, 256, 256], P('sp', None, 'env')
The draws below stay inside these ranges and needn't reach their ends.
All inputs are finite; a program needn't handle non-finite values.
Results may differ from the reference program's by a relative error of at most 0.002.
Values may be sent and summed in bfloat16 or wider, within the bound.
No kernel may reach another device: no remote copies, remote signals or barrier semaphores. Data moves between devices by JAX's collectives and lax.ppermute only.
A program may use at most 64 MiB of HBM per device.

```python
import math
import jax
import jax.numpy as jnp
from jax import lax

DESC = 512
SPB = 256
ZETA = 4
ENVIRONMENTS = 16384
SPARSE = 8192
N_SP = 32


centre_count = 16


def shared_centres(key):
    return jax.random.normal(jax.random.fold_in(key, 7), (centre_count, DESC), jnp.float32)


def mixed_rows(key, centres, jitter, second_high, jitter_low, jitter_high):
    row_count = jitter.shape[0]
    first = jax.random.randint(jax.random.fold_in(key, 1), (row_count,), 0, centre_count)
    step_by = jax.random.randint(jax.random.fold_in(key, 2), (row_count,), 1, centre_count)
    second = (first + step_by) % centre_count
    leading = jax.random.uniform(jax.random.fold_in(key, 3), (row_count, 1), jnp.float32, 0.5, 1.0)
    flips = jax.random.randint(jax.random.fold_in(key, 4), (row_count, 1), 0, 2)
    leading = leading * (2.0 * flips.astype(jnp.float32) - 1.0)
    second_weight = jax.random.uniform(jax.random.fold_in(key, 5), (row_count, 1), jnp.float32, -second_high, second_high)
    log_scale = jax.random.uniform(jax.random.fold_in(key, 6), (row_count, 1), jnp.float32, math.log(jitter_low), math.log(jitter_high))
    values = leading * centres[first] + second_weight * centres[second] + jnp.exp(log_scale) * jitter
    return jnp.clip(values, -6.0, 6.0).astype(jnp.bfloat16)


def draw_descriptors(key, part):
    centres = shared_centres(key)
    key = jax.random.fold_in(key, 11)
    jitter_key = jax.random.fold_in(key, 9)
    jitter = jax.random.normal(jitter_key, (ENVIRONMENTS, DESC), jnp.float32)
    return mixed_rows(key, centres, jitter, 0.8, 0.15, 0.5)


def draw_sparse_points(key, part):
    centres = shared_centres(key)
    key = jax.random.fold_in(key, 12)
    jitter_key = jax.random.fold_in(key, 9)
    jitter = jax.random.normal(jitter_key, (SPARSE, DESC), jnp.float32)
    return mixed_rows(key, centres, jitter, 0.8, 0.15, 0.5)


def setup_inputs(seed: int = 0) -> dict:
    keys = jax.random.split(jax.random.key(seed), 3)
    descriptors = draw_descriptors(jax.random.fold_in(keys[2], 71), 0)
    sparse_points = draw_sparse_points(jax.random.fold_in(keys[2], 71), 0)
    return dict(descriptors=descriptors, sparse_points=sparse_points)


def unit_rows(values):
    values = values.astype(jnp.float32)
    scale = lax.rsqrt(lax.optimization_barrier(jnp.sum(values * values, axis=1, keepdims=True)) + 1e-06)
    return (values * scale).astype(jnp.bfloat16)

def reference(descriptors, sparse_points):
    env_hat = unit_rows(descriptors)
    point_hat = unit_rows(sparse_points)
    products = lax.dot_general(point_hat, env_hat, (((1,), (1,)), ((), ())), preferred_element_type=jnp.float32)
    kernel = (4.0 * products ** ZETA).astype(jnp.bfloat16)
    blocks = kernel.reshape(N_SP, SPB, ENVIRONMENTS).astype(jnp.float32)
    band_list = []
    for offset in range(N_SP // 2 + 1):
        partner = jnp.roll(blocks, -offset, axis=0)
        band_list.append(jnp.einsum('snk,smk->snm', blocks, partner))
    return jnp.stack(band_list, axis=1) / jnp.float32(ENVIRONMENTS)
```

```python
import functools

import jax
import jax.numpy as jnp
from jax import lax
from jax.experimental import pallas as pl
from jax.experimental.pallas import tpu as pltpu
from jax.sharding import PartitionSpec as P


F32, BF16 = jnp.float32, jnp.bfloat16
NT = (((1,), (1,)), ((), ()))
NN = (((1,), (0,)), ((), ()))
VMEM_LIMIT = 48 * 1024 * 1024


def split_index(i):
    env, sp = divmod(i, 32)
    y_hi, x = divmod(env, 4)
    q, core = divmod(sp, 2)
    z, y_lo = divmod(q, 2)
    return y_hi, x, z, y_lo, core


def join_index(y_hi, x, z, y_lo, core):
    return ((y_hi % 2) * 4 + x % 4) * 32 + ((z % 8) * 2 + y_lo % 2) * 2 + core % 2


def fetch(value, source_of):
    pairs = []
    for i in range(256):
        pairs.append((join_index(*source_of(*split_index(i))), i))
    return lax.ppermute(value, ("env", "sp"), pairs)


def other_core(y_hi, x, z, y_lo, core):
    return y_hi, x, z, y_lo, 1 - core


def next_x(y_hi, x, z, y_lo, core):
    return y_hi, x + 1, z, y_lo, core


def previous_x(y_hi, x, z, y_lo, core):
    return y_hi, x - 1, z, y_lo, core


def next_z(y_hi, x, z, y_lo, core):
    return y_hi, x, z + 1, y_lo, core


def first_column(y_hi, x, z, y_lo, core):
    if x % 2 == 0:
        return y_hi, x, z + 1, y_lo, core
    y = (y_hi * 2 + y_lo + (1 if core == 0 else -1)) % 4
    return y // 2, x, z + y_lo, y % 2, core


def env_peer(flip, step):
    def source(y_hi, x, z, y_lo, core):
        return (y_hi + flip) % 2, x - step, z, y_lo, core

    return source


def unit(values):
    values = values.astype(F32)
    total = jnp.sum(values * values, axis=1, keepdims=True)
    return (values * lax.rsqrt(total + 1e-06)).astype(BF16)


def fourth(products):
    squares = products * products
    return (squares * squares).astype(BF16)


def own_kernel(chunk, own_env, near_a, near_b, far, own_points, sib_points, weight,
               env_hat, rows_k, own_out, sib_out):
    points = jnp.concatenate([unit(own_points[...]), unit(sib_points[...])], axis=0)
    gram = jnp.zeros((512, 256), F32)
    place = 0
    for ref in (own_env, near_a, near_b, far):
        for start in range(0, ref.shape[0], chunk):
            env = unit(ref[start:start + chunk, :])
            env_hat[place:place + chunk, :] = env
            k = fourth(lax.dot_general(points, env, NT, preferred_element_type=F32))
            rows_k[:, place:place + chunk] = k
            gram += lax.dot_general(k, k[:256], NT, preferred_element_type=F32)
            place += chunk
    gram = (gram * weight[...]).astype(BF16)
    own_out[...] = gram[:256]
    sib_out[...] = gram[256:]


def column_kernel(chunk, points, env_hat, rows_k, weight, own_out, sib_out):
    turned = unit(points[...]).T
    gram = jnp.zeros((512, 256), F32)
    for start in range(0, env_hat.shape[0], chunk):
        k = fourth(lax.dot_general(env_hat[start:start + chunk, :], turned, NN, preferred_element_type=F32))
        gram += lax.dot_general(rows_k[:, start:start + chunk], k, NN, preferred_element_type=F32)
    gram = (gram * weight[...]).astype(BF16)
    own_out[...] = gram[:256]
    sib_out[...] = gram[256:]


def pack_kernel(count, places, *refs):
    sources, outs = refs[:count], refs[count:]
    for r, out in enumerate(outs):
        start = pl.multiple_of(places[r] * 32, 32)
        for t, source in enumerate(sources):
            out[t] = source[pl.ds(start, 32), :]


def finish_kernel(flags, weights, *refs):
    pieces, out = refs[:8], refs[8]
    parity, core = flags[0], flags[1]
    same = jnp.zeros((9, 32, 256), F32)
    other = jnp.zeros((9, 32, 256), F32)
    for r in range(8):
        term = pieces[r][...].astype(F32) * weights[r][None, None, :]
        if r % 2 == 0:
            same += term
        else:
            other += term
    out[0] = jnp.where(parity == 0, same[0], other[0])
    same_odd = jnp.where(parity == core, 3, 1)
    for m in range(1, 5):
        out[4 * m - 2 * parity] = same[m]
        out[4 * m - 2 + 2 * parity] = other[m]
        out[4 * m - same_odd] = same[4 + m]
        out[4 * m - 4 + same_odd] = other[4 + m]


def spread(index):
    lanes = jnp.arange(256, dtype=jnp.int32)
    return 1.0 + ((lanes[None, :] + 64 * index[:, None]) % 256).astype(F32) / 256.0


def vmem_spec():
    return pl.BlockSpec(memory_space=pltpu.VMEM)


def smem_spec():
    return pl.BlockSpec(memory_space=pltpu.SMEM)


def shape(*dims, dtype=BF16):
    return jax.ShapeDtypeStruct(dims, dtype)


def call(body, out_shape, n_in, flops, bytes_accessed, smem=()):
    many = isinstance(out_shape, (tuple, list))
    return pl.pallas_call(
        body,
        out_shape=out_shape,
        in_specs=[smem_spec() if i in smem else vmem_spec() for i in range(n_in)],
        out_specs=[vmem_spec() for _ in out_shape] if many else vmem_spec(),
        compiler_params=pltpu.CompilerParams(vmem_limit_bytes=VMEM_LIMIT),
        cost_estimate=pl.CostEstimate(flops=flops, bytes_accessed=bytes_accessed, transcendentals=0),
    )


def on_device(descriptors, sparse_points):
    env, sp = lax.axis_index("env"), lax.axis_index("sp")
    y_hi, x, core = env // 4, env % 4, sp % 2
    parity = x % 2

    columns = [fetch(sparse_points, first_column)]
    for _ in range(3):
        columns.append(fetch(columns[-1], next_z))
    sib_points = fetch(sparse_points, other_core)
    low = lax.dynamic_slice_in_dim(descriptors, core * 512, 512, 0)
    high = lax.dynamic_slice_in_dim(descriptors, 1024 + core * 512, 512, 0)
    near_a, near_b = fetch(low, next_x), fetch(high, previous_x)
    far = fetch(jnp.concatenate([near_a, near_b], axis=0), other_core)

    group = (y_hi * 2 + x // 2)[None]
    weight = spread(group) * (16.0 / 16384.0)
    gram_pair = (shape(256, 256), shape(256, 256))
    env_hat, rows_k, own0, sib0 = call(
        functools.partial(own_kernel, 256),
        (shape(4096, 512), shape(512, 4096)) + gram_pair, 7, 2 * 1342177280, 1 << 24,
    )(descriptors, near_a, near_b, far, sparse_points, sib_points, weight)
    own, sib = [own0], [sib0]
    for points in columns:
        a, b = call(
            functools.partial(column_kernel, 512), gram_pair, 4, 2 * 1073741824, 1 << 23,
        )(points, env_hat, rows_k, weight)
        own.append(a)
        sib.append(b)

    late = jnp.logical_and(parity == 0, core == 1)
    for i in range(1, 5):
        own.append(fetch(jnp.where(late, sib[i - 1], sib[i]), other_core))

    turns = [(r // 4, r % 4) for r in range(8)]
    places = jnp.stack([((y_hi + flip) % 2) * 4 + (x + step) % 4 for flip, step in turns])
    packed = call(
        functools.partial(pack_kernel, 9), tuple(shape(9, 32, 256) for _ in range(8)), 10, 0, 1 << 21, (0,)
    )(places, *own)
    pieces = [packed[0]]
    for r in range(1, 8):
        pieces.append(fetch(packed[r], env_peer(*turns[r])))

    groups = jnp.stack([((y_hi + flip) % 2) * 2 + ((x - step) % 4) // 2 for flip, step in turns])
    flags = jnp.stack([parity, core])
    out = call(finish_kernel, shape(17, 32, 256, dtype=F32), 10, 0, 1 << 21, (0,))(
        flags, 1.0 / spread(groups), *pieces
    )
    return out[None]


def solution(mesh):
    placed = (P("env", None), P("sp", None))
    return jax.shard_map(
        on_device, mesh=mesh, in_specs=placed, out_specs=P("sp", None, "env", None), check_vma=False
    )
```

```python
import functools

import jax
import jax.numpy as jnp
from jax import lax
from jax.experimental import pallas as pl
from jax.experimental.pallas import tpu as pltpu
from jax.sharding import PartitionSpec as P


F32, BF16 = jnp.float32, jnp.bfloat16
NT = (((1,), (1,)), ((), ()))
VMEM_LIMIT = 24 * 1024 * 1024


def split_index(i):
    env, sp = divmod(i, 32)
    y_hi, x = divmod(env, 4)
    q, core = divmod(sp, 2)
    z, y_lo = divmod(q, 2)
    return y_hi, x, z, y_lo, core


def join_index(y_hi, x, z, y_lo, core):
    return ((y_hi % 2) * 4 + x % 4) * 32 + ((z % 8) * 2 + y_lo % 2) * 2 + core % 2


def fetch(value, source_of):
    pairs = [(join_index(*source_of(*split_index(i))), i) for i in range(256)]
    return lax.ppermute(value, ("env", "sp"), pairs)


def other_core(y_hi, x, z, y_lo, core):
    return y_hi, x, z, y_lo, 1 - core


def near_x(y_hi, x, z, y_lo, core):
    return y_hi, x + 1 - 2 * core, z, y_lo, core


def column(first):
    def source(y_hi, x, z, y_lo, core):
        m = first + y_hi
        if x % 2 == 0:
            return y_hi, x, z + m, y_lo, core
        y = (y_hi * 2 + y_lo + 1 - 2 * core) % 4
        return y // 2, x, z + y_lo + m - 1, y % 2, core

    return source


def sharer(flip, step):
    def source(y_hi, x, z, y_lo, core):
        return (y_hi + flip) % 2, x + step, z, y_lo, core

    return source


def unit(values):
    values = values.astype(F32)
    total = jnp.sum(values * values, axis=1, keepdims=True)
    return (values * lax.rsqrt(total + 1e-06)).astype(BF16)


def fourth(products):
    squares = products * products
    return (squares * squares).astype(BF16)


def dot(a, b):
    return lax.dot_general(a, b, NT, preferred_element_type=F32)


CHUNK = 512


def rows_of(points, raw, env_hat, rows_k):
    place = 0
    for ref in raw:
        for start in range(0, ref.shape[0], CHUNK):
            env = unit(ref[start:start + CHUNK, :])
            env_hat[place:place + CHUNK, :] = env
            rows_k[:, place:place + CHUNK] = fourth(dot(points, env))
            place += CHUNK


def own_kernel(own_env, own_points, sib_points, env_hat, rows_k, points_hat, gram):
    points_hat[:256, :] = unit(own_points[...])
    points_hat[256:, :] = unit(sib_points[...])
    rows_of(points_hat[...], (own_env,), env_hat, rows_k)
    gram[...] = dot(rows_k[...], rows_k[:256, :])


def more_kernel(near, far, points_hat, gram, weight, env_hat, rows_k, own_out, sib_out):
    rows_of(points_hat[...], (near, far), env_hat, rows_k)
    total = (gram[...] + dot(rows_k[...], rows_k[:256, :])) * weight[...]
    total = total.astype(BF16)
    own_out[...] = total[:256]
    sib_out[...] = total[256:]


def quarter_kernel(first, second, out):
    out[:128, :] = unit(first[...])
    out[128:, :] = unit(second[...])


def column_kernel(points, env_a, env_b, rows_a, rows_b, weight, own_out, sib_out, kept):
    half = env_a.shape[0]
    for place in range(0, 2 * half, CHUNK):
        env, start = (env_a, place) if place < half else (env_b, place - half)
        kept[:, place:place + CHUNK] = fourth(dot(points[...], env[start:start + CHUNK, :]))
    total = dot(rows_a[...], kept[:, :half]) + dot(rows_b[...], kept[:, half:])
    total = (total * weight[...]).astype(BF16)
    own_out[...] = total[:256]
    sib_out[...] = total[256:]


def pack_kernel(flags, *refs):
    own, swapped, out = refs[:5], refs[5:10], refs[10]
    y_hi, half, late = flags[0], flags[1], flags[2]
    for e in range(8):
        rows = slice(32 * e, 32 * e + 32)
        out[e, 0] = own[0][rows, :]

    @pl.when(late == 1)
    def _():
        for e in range(8):
            out[e, 5] = swapped[0][32 * e:32 * e + 32, :]

    for v in range(4):
        which = y_hi if v < 2 else 1 - y_hi
        side = half if v % 2 == 0 else 1 - half
        lanes = pl.ds(pl.multiple_of(side * 128, 128), 128)
        for part in range(2):
            m = 1 + 2 * part + which
            cols = slice(128 * part, 128 * part + 128)
            for e in range(8):
                out[e, m, :, lanes] = own[1 + v][32 * e:32 * e + 32, cols]

            @pl.when(m + late <= 4)
            def _(v=v, m=m, cols=cols, lanes=lanes):
                for e in range(8):
                    out[e, 4 + m + late, :, lanes] = swapped[1 + v][32 * e:32 * e + 32, cols]


def finish_kernel(flags, weights, pieces, out):
    core = flags[0]
    even, odd = None, None
    for e in range(0, 8, 2):
        a = pieces[e].astype(F32) * weights[e][None, None, :]
        b = pieces[e + 1].astype(F32) * weights[e + 1][None, None, :]
        even, odd = (a, b) if even is None else (even + a, odd + b)
    out[0] = even[0]
    shift = 2 * core
    for m in range(1, 5):
        out[4 * m] = even[m]
        out[4 * m - 2] = odd[m]
        out[4 * m - 3 + shift] = even[4 + m]
        out[4 * m - 1 - shift] = odd[4 + m]


def spread(index, lanes=None):
    lanes = jnp.arange(256, dtype=jnp.int32) if lanes is None else lanes
    return 1.0 + ((lanes[None, :] + 64 * index[:, None]) % 256).astype(F32) / 256.0


def vmem_spec():
    return pl.BlockSpec(memory_space=pltpu.VMEM)


def smem_spec():
    return pl.BlockSpec(memory_space=pltpu.SMEM)


def shape(*dims, dtype=BF16):
    return jax.ShapeDtypeStruct(dims, dtype)


def call(body, out_shape, n_in, flops, bytes_accessed, smem=(), scratch=()):
    many = isinstance(out_shape, (tuple, list))
    return pl.pallas_call(
        body,
        out_shape=out_shape,
        in_specs=[smem_spec() if i in smem else vmem_spec() for i in range(n_in)],
        out_specs=[vmem_spec() for _ in out_shape] if many else vmem_spec(),
        scratch_shapes=scratch,
        compiler_params=pltpu.CompilerParams(vmem_limit_bytes=VMEM_LIMIT),
        cost_estimate=pl.CostEstimate(flops=flops, bytes_accessed=bytes_accessed, transcendentals=0),
    )


def on_device(descriptors, sparse_points):
    env, sp = lax.axis_index("env"), lax.axis_index("sp")
    y_hi, x, core = env // 4, env % 4, sp % 2
    half = x // 2

    sib_points = fetch(sparse_points, other_core)
    piece = lax.dynamic_slice_in_dim(sparse_points, half * 128, 128, 0)
    first, second = fetch(piece, column(1)), fetch(piece, column(3))
    near = fetch(lax.dynamic_slice_in_dim(descriptors, core * 1024, 1024, 0), near_x)

    env_a, rows_a, points_hat, gram = call(
        own_kernel,
        (shape(2048, 512), shape(512, 2048), shape(512, 512), shape(512, 256, dtype=F32)),
        3, 2 * 805306368, 1 << 23,
    )(descriptors, sparse_points, sib_points)
    first, second, near, env_a, rows_a, points_hat, gram = lax.optimization_barrier(
        (first, second, near, env_a, rows_a, points_hat, gram)
    )

    quarter = call(quarter_kernel, shape(256, 512), 2, 1 << 20, 1 << 19)(first, second)
    quarters = [quarter] + [fetch(quarter, sharer(*turn)) for turn in ((0, 2), (1, 0), (1, 2))]
    far = fetch(near, other_core)

    group = (y_hi * 2 + half)[None]
    weight = spread(group) * (16.0 / 16384.0)
    pair = (shape(256, 256), shape(256, 256))
    env_b, rows_b, own0, sib0 = call(
        more_kernel, (shape(2048, 512), shape(512, 2048)) + pair, 5, 2 * 805306368, 1 << 23
    )(near, far, points_hat, gram, weight)
    lanes = jnp.arange(256, dtype=jnp.int32) % 128
    sides = [spread(group, lanes + 128 * side) * (16.0 / 16384.0) for side in (half, 1 - half)]
    own, sib = [own0], [sib0]
    for v, points in enumerate(quarters):
        a, b = call(
            column_kernel, pair, 6, 2 * 1073741824, 1 << 23, scratch=(pltpu.VMEM((256, 4096), BF16),)
        )(points, env_a, env_b, rows_a, rows_b, sides[v % 2])
        own.append(a)
        sib.append(b)

    swapped = [fetch(value, other_core) for value in sib]
    late = jnp.logical_and(x % 2 == 0, core == 0).astype(jnp.int32)
    packed = call(pack_kernel, shape(8, 9, 32, 256), 11, 0, 1 << 21, (0,))(
        jnp.stack([y_hi, half, late]), *own, *swapped
    )
    pieces = lax.all_to_all(packed, "env", 0, 0, tiled=True)

    sources = jnp.arange(8, dtype=jnp.int32)
    weights = 1.0 / spread((sources // 4) * 2 + (sources % 4) // 2)
    out = call(finish_kernel, shape(17, 32, 256, dtype=F32), 3, 0, 1 << 21, (0,))(core[None], weights, pieces)
    return out[None]


def solution(mesh):
    placed = (P("env", None), P("sp", None))
    return jax.shard_map(
        on_device, mesh=mesh, in_specs=placed, out_specs=P("sp", None, "env", None), check_vma=False
    )
```

```python
import functools

import jax
import jax.numpy as jnp
from jax import lax
from jax.experimental import pallas as pl
from jax.experimental.pallas import tpu as pltpu
from jax.sharding import PartitionSpec as P


F32, BF16 = jnp.float32, jnp.bfloat16
NT = (((1,), (1,)), ((), ()))
VMEM_LIMIT = 20 * 1024 * 1024


def split_index(i):
    env, sp = divmod(i, 32)
    y_hi, x = divmod(env, 4)
    q, core = divmod(sp, 2)
    z, y_lo = divmod(q, 2)
    return y_hi, x, z, y_lo, core


def join_index(y_hi, x, z, y_lo, core):
    return ((y_hi % 2) * 4 + x % 4) * 32 + ((z % 8) * 2 + y_lo % 2) * 2 + core % 2


def fetch(value, source_of):
    pairs = [(join_index(*source_of(*split_index(i))), i) for i in range(256)]
    return lax.ppermute(value, ("env", "sp"), pairs)


def other_core(y_hi, x, z, y_lo, core):
    return y_hi, x, z, y_lo, 1 - core


def near_x(y_hi, x, z, y_lo, core):
    return y_hi, x + 1 - 2 * core, z, y_lo, core


def next_z(y_hi, x, z, y_lo, core):
    return y_hi, x, z + 1, y_lo, core


def first_column(y_hi, x, z, y_lo, core):
    if x % 2 == 0:
        return y_hi, x, z + 1, y_lo, core
    y = (y_hi * 2 + y_lo + 1 - 2 * core) % 4
    return y // 2, x, z + y_lo, y % 2, core


def unit(values):
    values = values.astype(F32)
    total = jnp.sum(values * values, axis=1, keepdims=True)
    return (values * lax.rsqrt(total + 1e-06)).astype(BF16)


def fourth(products):
    squares = products * products
    return (squares * squares).astype(BF16)


def dot(a, b):
    return lax.dot_general(a, b, NT, preferred_element_type=F32)


CHUNK = 512


def weight_row():
    env = lax.axis_index("env")
    group = (env // 4) * 2 + (env % 4) // 2
    lanes = lax.broadcasted_iota(jnp.int32, (1, 256), 1)
    return (1.0 + ((lanes + 64 * group) % 256).astype(F32) / 256.0) * (16.0 / 16384.0)


def source_weight(e):
    group = (e // 4) * 2 + (e % 4) // 2
    lanes = lax.broadcasted_iota(jnp.int32, (1, 256), 1)
    return 1.0 / (1.0 + ((lanes + 64 * group) % 256).astype(F32) / 256.0)


def rows_of(points, raw, env_hat, rows_k):
    place = 0
    for ref in raw:
        for start in range(0, ref.shape[0], CHUNK):
            env = unit(ref[start:start + CHUNK, :])
            env_hat[place:place + CHUNK, :] = env
            rows_k[:, place:place + CHUNK] = fourth(dot(points, env))
            place += CHUNK


def slice_kernel(descriptors, first_out, second_out, sems):
    start = pl.multiple_of((lax.axis_index("sp") % 2) * 1024, 1024)
    copies = []
    for i, out in enumerate((first_out, second_out)):
        copies.append(pltpu.make_async_copy(descriptors.at[pl.ds(start + 512 * i, 512), :], out, sems.at[i]))
        copies[i].start()
    for copy in copies:
        copy.wait()


def own_kernel(own_env, own_points, sib_points, env_hat, rows_k, gram, points_hat):
    points_hat[:256, :] = unit(own_points[...])
    points_hat[256:, :] = unit(sib_points[...])
    rows_of(points_hat[...], (own_env,), env_hat, rows_k)
    gram[...] = dot(rows_k[...], rows_k[:256, :])


def more_kernel(near, far, points_hat, gram, env_hat, rows_k, gram_out):
    rows_of(points_hat[...], (near, far), env_hat, rows_k)
    gram_out[...] = gram[...] + dot(rows_k[...], rows_k[:256, :])


def last_kernel(near, far, points_hat, gram, env_hat, rows_k, own_out, sib_out):
    rows_of(points_hat[...], (near, far), env_hat, rows_k)
    total = ((gram[...] + dot(rows_k[...], rows_k[:256, :])) * weight_row()).astype(BF16)
    own_out[...] = total[:256]
    sib_out[...] = total[256:]


def column_kernel(points, *refs):
    envs, rows, own_out, sib_out, kept = refs[:3], refs[3:6], refs[6], refs[7], refs[8]
    point_hat = unit(points[...])
    total, place = None, 0
    for env in envs:
        for start in range(0, env.shape[0], CHUNK):
            kept[:, place:place + CHUNK] = fourth(dot(point_hat, env[start:start + CHUNK, :]))
            place += CHUNK
    place = 0
    for row in rows:
        term = dot(row[...], kept[:, place:place + row.shape[1]])
        total = term if total is None else total + term
        place += row.shape[1]
    total = (total * weight_row()).astype(BF16)
    own_out[...] = total[:256]
    sib_out[...] = total[256:]


def pack_kernel(*refs):
    own, swapped, out = refs[:5], refs[5:10], refs[10]
    even_x = lax.axis_index("env") % 2 == 0
    shift = jnp.logical_and(even_x, lax.axis_index("sp") % 2 == 0)
    for e in range(8):
        rows = slice(32 * e, 32 * e + 32)
        for m in range(5):
            out[e, m] = own[m][rows, :]
        for m in range(1, 5):
            out[e, 4 + m] = jnp.where(shift, swapped[m - 1][rows, :], swapped[m][rows, :])


def finish_kernel(pieces, out):
    core = lax.axis_index("sp") % 2

    def total(parity, slot):
        value = None
        for e in range(parity, 8, 2):
            term = pieces[e, slot].astype(F32) * source_weight(e)
            value = term if value is None else value + term
        return value

    out[0] = total(0, 0)
    for m in range(1, 5):
        out[4 * m] = total(0, m)
        out[4 * m - 2] = total(1, m)
        out[4 * m - 3 + 2 * core] = total(0, 4 + m)
        out[4 * m - 1 - 2 * core] = total(1, 4 + m)


def vmem_spec():
    return pl.BlockSpec(memory_space=pltpu.VMEM)


def shape(*dims, dtype=BF16):
    return jax.ShapeDtypeStruct(dims, dtype)


def call(body, out_shape, n_in, flops, bytes_accessed, scratch=(), in_place=False):
    many = isinstance(out_shape, (tuple, list))
    return pl.pallas_call(
        body,
        out_shape=out_shape,
        in_specs=[pl.BlockSpec(memory_space=pl.ANY) if in_place else vmem_spec() for _ in range(n_in)],
        out_specs=[vmem_spec() for _ in out_shape] if many else vmem_spec(),
        scratch_shapes=scratch,
        compiler_params=pltpu.CompilerParams(vmem_limit_bytes=VMEM_LIMIT),
        cost_estimate=pl.CostEstimate(flops=flops, bytes_accessed=bytes_accessed, transcendentals=0),
    )


def on_device(descriptors, sparse_points):
    barrier = lax.optimization_barrier

    def rows(body, envs, sums, n_in, *args):
        return call(body, (shape(envs, 512), shape(512, envs)) + sums, n_in, envs * 786432, envs << 12)(*args)

    gram_shape = shape(512, 256, dtype=F32)
    pair = (shape(256, 256), shape(256, 256))

    column = fetch(sparse_points, first_column)
    sib_points = fetch(sparse_points, other_core)
    low, high = call(
        slice_kernel, (shape(512, 512), shape(512, 512)), 1, 0, 1 << 21, (pltpu.SemaphoreType.DMA((2,)),), True
    )(descriptors)
    near = fetch(low, near_x)
    env_a, rows_a, gram, points_hat = rows(
        own_kernel, 2048, (gram_shape, shape(512, 512)), 3, descriptors, sparse_points, sib_points
    )
    columns = [column]
    column, near, high, env_a, rows_a, gram, points_hat = barrier(
        (column, near, high, env_a, rows_a, gram, points_hat)
    )

    far = fetch(near, other_core)
    columns.append(fetch(column, next_z))
    near_b = fetch(high, near_x)
    env_b, rows_b, gram = rows(more_kernel, 1024, (gram_shape,), 4, near, far, points_hat, gram)
    column, near_b, env_b, rows_b, gram = barrier((columns[1], near_b, env_b, rows_b, gram))

    columns.append(fetch(column, next_z))
    env_c, rows_c, own, sib = rows(
        last_kernel, 1024, pair, 4, near_b, fetch(near_b, other_core), points_hat, gram
    )
    owns, sibs = [own], [sib]

    def take(points):
        own, sib = call(
            column_kernel, pair, 7, 2 * 1073741824, 1 << 23, (pltpu.VMEM((256, 4096), BF16),)
        )(points, env_a, env_b, env_c, rows_a, rows_b, rows_c)
        owns.append(own)
        sibs.append(sib)

    take(columns[0])
    column, owns[1], sibs[1] = barrier((columns[2], owns[1], sibs[1]))

    columns.append(fetch(column, next_z))
    for points in columns[1:]:
        take(points)

    swapped = [fetch(sib, other_core) for sib in sibs]
    packed = call(pack_kernel, shape(8, 9, 32, 256), 10, 0, 1 << 21)(*owns, *swapped)
    pieces = lax.all_to_all(packed, "env", 0, 0, tiled=True)
    return call(finish_kernel, shape(17, 32, 256, dtype=F32), 1, 0, 1 << 21)(pieces)[None]


def solution(mesh):
    placed = (P("env", None), P("sp", None))
    return jax.shard_map(
        on_device, mesh=mesh, in_specs=placed, out_specs=P("sp", None, "env", None), check_vma=False
    )
```

```python
import functools

import jax
import jax.numpy as jnp
from jax import lax
from jax.experimental import pallas as pl
from jax.experimental.pallas import tpu as pltpu
from jax.sharding import PartitionSpec as P


F32, BF16 = jnp.float32, jnp.bfloat16
NT = (((1,), (1,)), ((), ()))
VMEM_LIMIT = 20 * 1024 * 1024


def split_index(i):
    env, sp = divmod(i, 32)
    y_hi, x = divmod(env, 4)
    q, core = divmod(sp, 2)
    z, y_lo = divmod(q, 2)
    return y_hi, x, z, y_lo, core


def join_index(y_hi, x, z, y_lo, core):
    return ((y_hi % 2) * 4 + x % 4) * 32 + ((z % 8) * 2 + y_lo % 2) * 2 + core % 2


def fetch(value, source_of):
    pairs = [(join_index(*source_of(*split_index(i))), i) for i in range(256)]
    return lax.ppermute(value, ("env", "sp"), pairs)


def other_core(y_hi, x, z, y_lo, core):
    return y_hi, x, z, y_lo, 1 - core


def y_partner(y_hi, x, z, y_lo, core):
    return 1 - y_hi, x, z, 1 - y_lo, core


def column(first):
    def source(y_hi, x, z, y_lo, core):
        m = first + x // 2
        if y_hi == 0:
            return y_hi, x, z + m, y_lo, core
        return y_hi, x, z + y_lo + m - 1, 1 - y_lo, core

    return source


def along_x(step):
    def source(y_hi, x, z, y_lo, core):
        return y_hi, x + step, z, y_lo, core

    return source


def unit(values):
    values = values.astype(F32)
    total = jnp.sum(values * values, axis=1, keepdims=True)
    return (values * lax.rsqrt(total + 1e-06)).astype(BF16)


def fourth(products):
    squares = products * products
    return (squares * squares).astype(BF16)


def dot(a, b):
    return lax.dot_general(a, b, NT, preferred_element_type=F32)


CHUNK = 512


def spread(group):
    lanes = lax.broadcasted_iota(jnp.int32, (1, 256), 1)
    return 1.0 + ((lanes + 64 * group) % 256).astype(F32) / 256.0


def weight_row():
    return spread(lax.axis_index("env") % 4) * (16.0 / 16384.0)


def rows_of(points, raw, env_hat, rows_k):
    place = 0
    for ref in raw:
        for start in range(0, ref.shape[0], CHUNK):
            env = unit(ref[start:start + CHUNK, :])
            env_hat[place:place + CHUNK, :] = env
            rows_k[:, place:place + CHUNK] = fourth(dot(points, env))
            place += CHUNK


def piece_kernel(points, out, sem):
    start = pl.multiple_of((lax.axis_index("env") % 2) * 128, 128)
    copy = pltpu.make_async_copy(points.at[pl.ds(start, 128), :], out, sem)
    copy.start()
    copy.wait()


def slice_kernel(descriptors, first_out, second_out, sems):
    start = pl.multiple_of((lax.axis_index("sp") % 2) * 1024, 1024)
    copies = []
    for i, out in enumerate((first_out, second_out)):
        copies.append(pltpu.make_async_copy(descriptors.at[pl.ds(start + 512 * i, 512), :], out, sems.at[i]))
        copies[i].start()
    for copy in copies:
        copy.wait()


def own_kernel(own_env, own_points, sib_points, env_hat, rows_k, gram, points_hat):
    points_hat[:256, :] = unit(own_points[...])
    points_hat[256:, :] = unit(sib_points[...])
    rows_of(points_hat[...], (own_env,), env_hat, rows_k)
    gram[...] = dot(rows_k[...], rows_k[:256, :])


def more_kernel(near, far, points_hat, gram, env_hat, rows_k, gram_out):
    rows_of(points_hat[...], (near, far), env_hat, rows_k)
    gram_out[...] = gram[...] + dot(rows_k[...], rows_k[:256, :])


def quarter_kernel(first, second, out):
    out[:128, :] = unit(first[...])
    out[128:, :] = unit(second[...])


def column_kernel(points, env_a, env_b, rows_a, rows_b, gram, kept):
    total, place = None, 0
    for env in (env_a, env_b):
        for start in range(0, env.shape[0], CHUNK):
            kept[:, place:place + CHUNK] = fourth(dot(points[...], env[start:start + CHUNK, :]))
            place += CHUNK
    size = env_a.shape[0]
    gram[...] = dot(rows_a[...], kept[:, :size]) + dot(rows_b[...], kept[:, size:])


def last_kernel(near, far, points_hat, *refs):
    grams, quarters, own_out, sib_out, env_hat, rows_k, kept = refs[:5], refs[5:9], *refs[9:]
    rows_of(points_hat[...], (near, far), env_hat, rows_k)
    weight = weight_row()
    for t in range(5):
        if t == 0:
            columns = rows_k[:256, :]
        else:
            for start in range(0, env_hat.shape[0], CHUNK):
                kept[:, start:start + CHUNK] = fourth(dot(quarters[t - 1][...], env_hat[start:start + CHUNK, :]))
            columns = kept[...]
        total = ((grams[t][...] + dot(rows_k[...], columns)) * weight).astype(BF16)
        own_out[t] = total[:256]
        sib_out[t] = total[256:]


def pack_kernel(own, swapped, out):
    x = lax.axis_index("env") % 4
    shift = jnp.logical_and(lax.axis_index("env") < 4, lax.axis_index("sp") % 2 == 0)
    for e in range(8):
        rows = slice(32 * e, 32 * e + 32)
        out[e, 0] = own[0, rows, :]
        for v in range(4):
            out[e, 1 + v] = own[1 + v, rows, :]
            out[e, 5 + v, :, :128] = swapped[1 + v, rows, :128]
            start = jnp.where(x % 2 == v % 2, swapped[0, rows, :128], swapped[0, rows, 128:])
            instead = jnp.logical_and(shift, (x + v) % 4 >= 2)
            out[e, 5 + v, :, 128:] = jnp.where(instead, start, swapped[1 + v, rows, 128:])


def finish_kernel(pieces, out):
    core = lax.axis_index("sp") % 2
    inverse = [1.0 / spread(x) for x in range(4)]

    def total(odd, which, side, base, lanes, weight_lanes):
        value = None
        for x in range(4):
            slot = base + (2 * which + side - x) % 4
            term = pieces[4 * odd + x, slot, :, lanes].astype(F32) * inverse[x][:, weight_lanes]
            value = term if value is None else value + term
        return value

    value = None
    for x in range(4):
        term = pieces[x, 0].astype(F32) * inverse[x]
        value = term if value is None else value + term
    out[0] = value
    for m in range(1, 5):
        which, part = (m - 1) % 2, (m - 1) // 2
        lanes = slice(128 * part, 128 * part + 128)
        for side in range(2):
            place = slice(128 * side, 128 * side + 128)
            out[4 * m, :, place] = total(0, which, side, 1, lanes, lanes)
            out[4 * m - 2, :, place] = total(1, which, side, 1, lanes, lanes)
            out[4 * m - 1 - 2 * core, :, place] = total(1, which, side, 5, lanes, lanes)
            if m < 4:
                out[4 * m + 1 - 2 * core, :, place] = total(0, which, side, 5, lanes, lanes)
            else:

                @pl.when(core == 0)
                def _(which=which, side=side, lanes=lanes, place=place):
                    out[1, :, place] = total(0, which, side, 5, lanes, place)

                @pl.when(core == 1)
                def _(which=which, side=side, lanes=lanes, place=place):
                    out[15, :, place] = total(0, which, side, 5, lanes, lanes)


def vmem_spec():
    return pl.BlockSpec(memory_space=pltpu.VMEM)


def shape(*dims, dtype=BF16):
    return jax.ShapeDtypeStruct(dims, dtype)


def call(body, out_shape, n_in, flops, bytes_accessed, scratch=(), in_place=False):
    many = isinstance(out_shape, (tuple, list))
    return pl.pallas_call(
        body,
        out_shape=out_shape,
        in_specs=[pl.BlockSpec(memory_space=pl.ANY) if in_place else vmem_spec() for _ in range(n_in)],
        out_specs=[vmem_spec() for _ in out_shape] if many else vmem_spec(),
        scratch_shapes=scratch,
        compiler_params=pltpu.CompilerParams(vmem_limit_bytes=VMEM_LIMIT),
        cost_estimate=pl.CostEstimate(flops=flops, bytes_accessed=bytes_accessed, transcendentals=0),
    )


def on_device(descriptors, sparse_points):
    barrier = lax.optimization_barrier

    def rows(body, envs, sums, n_in, *args):
        return call(body, (shape(envs, 512), shape(512, envs)) + sums, n_in, envs * 786432, envs << 12)(*args)

    gram_shape = shape(512, 256, dtype=F32)

    sib_points = fetch(sparse_points, other_core)
    piece = call(piece_kernel, shape(128, 512), 1, 0, 1 << 18, (pltpu.SemaphoreType.DMA,), True)(sparse_points)
    first, second = fetch(piece, column(1)), fetch(piece, column(3))
    low, high = call(
        slice_kernel, (shape(512, 512), shape(512, 512)), 1, 0, 1 << 21, (pltpu.SemaphoreType.DMA((2,)),), True
    )(descriptors)
    near = fetch(low, y_partner)
    env_a, rows_a, gram, points_hat = rows(
        own_kernel, 2048, (gram_shape, shape(512, 512)), 3, descriptors, sparse_points, sib_points
    )
    first, second, near, high, env_a, rows_a, gram, points_hat = barrier(
        (first, second, near, high, env_a, rows_a, gram, points_hat)
    )

    near_b = fetch(high, y_partner)
    quarter = call(quarter_kernel, shape(256, 512), 2, 1 << 20, 1 << 19)(first, second)
    quarters = [quarter] + [fetch(quarter, along_x(step)) for step in range(1, 4)]
    env_b, rows_b, gram = rows(more_kernel, 1024, (gram_shape,), 4, near, fetch(near, other_core), points_hat, gram)
    grams = [gram]
    for points in quarters:
        grams.append(
            call(column_kernel, gram_shape, 5, 2 * 805306368, 1 << 23, (pltpu.VMEM((256, 3072), BF16),))(
                points, env_a, env_b, rows_a, rows_b
            )
        )
    near_b, grams[1], grams[2] = barrier((near_b, grams[1], grams[2]))
    scratch = (pltpu.VMEM((1024, 512), BF16), pltpu.VMEM((512, 1024), BF16), pltpu.VMEM((256, 1024), BF16))
    own, sib = call(last_kernel, (shape(5, 256, 256), shape(5, 256, 256)), 12, 2 * 1744830464, 1 << 23, scratch)(
        near_b, fetch(near_b, other_core), points_hat, *grams, *quarters
    )

    packed = call(pack_kernel, shape(8, 9, 32, 256), 2, 0, 1 << 21)(own, fetch(sib, other_core))
    pieces = lax.all_to_all(packed, "env", 0, 0, tiled=True)
    return call(finish_kernel, shape(17, 32, 256, dtype=F32), 1, 0, 1 << 21)(pieces)[None]


def solution(mesh):
    placed = (P("env", None), P("sp", None))
    return jax.shard_map(
        on_device, mesh=mesh, in_specs=placed, out_specs=P("sp", None, "env", None), check_vma=False
    )
```

```python
import functools

import jax
import jax.numpy as jnp
from jax import lax
from jax.experimental import pallas as pl
from jax.experimental.pallas import tpu as pltpu
from jax.sharding import PartitionSpec as P


F32, BF16 = jnp.float32, jnp.bfloat16
NT = (((1,), (1,)), ((), ()))
VMEM_LIMIT = 20 * 1024 * 1024


def split_index(i):
    env, sp = divmod(i, 32)
    y_hi, x = divmod(env, 4)
    q, core = divmod(sp, 2)
    z, y_lo = divmod(q, 2)
    return y_hi, x, z, y_lo, core


def join_index(y_hi, x, z, y_lo, core):
    return ((y_hi % 2) * 4 + x % 4) * 32 + ((z % 8) * 2 + y_lo % 2) * 2 + core % 2


def fetch(value, source_of):
    pairs = [(join_index(*source_of(*split_index(i))), i) for i in range(256)]
    return lax.ppermute(value, ("env", "sp"), pairs)


def other_core(y_hi, x, z, y_lo, core):
    return y_hi, x, z, y_lo, 1 - core


def y_partner(y_hi, x, z, y_lo, core):
    return 1 - y_hi, x, z, 1 - y_lo, core


def column(first):
    def source(y_hi, x, z, y_lo, core):
        m = first + x // 2
        if y_hi == 0:
            return y_hi, x, z + m, y_lo, core
        return y_hi, x, z + y_lo + m - 1, 1 - y_lo, core

    return source


def along_x(step):
    def source(y_hi, x, z, y_lo, core):
        return y_hi, x + step, z, y_lo, core

    return source


def unit(values):
    values = values.astype(F32)
    total = jnp.sum(values * values, axis=1, keepdims=True)
    return (values * lax.rsqrt(total + 1e-06)).astype(BF16)


def fourth(products):
    squares = products * products
    return (squares * squares).astype(BF16)


def dot(a, b):
    return lax.dot_general(a, b, NT, preferred_element_type=F32)


FIRST = 768


def chunks(rows):
    return [(start, min(512, rows - start)) for start in range(0, rows, 512)]


def spread(group):
    lanes = lax.broadcasted_iota(jnp.int32, (1, 256), 1)
    return 1.0 + ((lanes + 64 * group) % 256).astype(F32) / 256.0


def weight_row():
    return spread(lax.axis_index("env") % 4) * (16.0 / 16384.0)


def rows_of(points, raw, env_hat, rows_k):
    place = 0
    for ref in raw:
        for start, size in chunks(ref.shape[0]):
            env = unit(ref[start:start + size, :])
            env_hat[place:place + size, :] = env
            rows_k[:, place:place + size] = fourth(dot(points, env))
            place += size


def piece_kernel(points, out):
    start = pl.multiple_of((lax.axis_index("env") % 2) * 128, 128)
    out[...] = points[pl.ds(start, 128), :]


def slice_kernel(descriptors, first_out, second_out):
    half = pl.multiple_of((lax.axis_index("sp") % 2) * 1024, 1024)
    first_out[...] = descriptors[pl.ds(half, FIRST), :]
    second_out[...] = descriptors[pl.ds(half + FIRST, 1024 - FIRST), :]


def own_kernel(own_env, own_points, sib_points, env_hat, rows_k, gram, points_hat):
    points_hat[:256, :] = unit(own_points[...])
    points_hat[256:, :] = unit(sib_points[...])
    rows_of(points_hat[...], (own_env,), env_hat, rows_k)
    gram[...] = dot(rows_k[...], rows_k[:256, :])


def more_kernel(near, far, points_hat, gram, env_hat, rows_k, gram_out):
    rows_of(points_hat[...], (near, far), env_hat, rows_k)
    gram_out[...] = gram[...] + dot(rows_k[...], rows_k[:256, :])


def quarter_kernel(first, second, out):
    out[:128, :] = unit(first[...])
    out[128:, :] = unit(second[...])


def column_kernel(points, env_a, env_b, rows_a, rows_b, gram, kept):
    total, place = None, 0
    for env in (env_a, env_b):
        for start, size in chunks(env.shape[0]):
            kept[:, place:place + size] = fourth(dot(points[...], env[start:start + size, :]))
            place += size
    size = env_a.shape[0]
    gram[...] = dot(rows_a[...], kept[:, :size]) + dot(rows_b[...], kept[:, size:])


def last_kernel(near, far, points_hat, *refs):
    grams, quarters, own_out, sib_out, env_hat, rows_k, kept = refs[:5], refs[5:9], *refs[9:]
    rows_of(points_hat[...], (near, far), env_hat, rows_k)
    weight = weight_row()
    for t in range(5):
        if t == 0:
            columns = rows_k[:256, :]
        else:
            for start, size in chunks(env_hat.shape[0]):
                kept[:, start:start + size] = fourth(dot(quarters[t - 1][...], env_hat[start:start + size, :]))
            columns = kept[...]
        total = ((grams[t][...] + dot(rows_k[...], columns)) * weight).astype(BF16)
        own_out[t] = total[:256]
        sib_out[t] = total[256:]


def pack_kernel(own, swapped, out):
    x = lax.axis_index("env") % 4
    shift = jnp.logical_and(lax.axis_index("env") < 4, lax.axis_index("sp") % 2 == 0)
    for e in range(8):
        rows = slice(32 * e, 32 * e + 32)
        out[e, 0] = own[0, rows, :]
        for v in range(4):
            out[e, 1 + v] = own[1 + v, rows, :]
            out[e, 5 + v, :, :128] = swapped[1 + v, rows, :128]
            start = jnp.where(x % 2 == v % 2, swapped[0, rows, :128], swapped[0, rows, 128:])
            instead = jnp.logical_and(shift, (x + v) % 4 >= 2)
            out[e, 5 + v, :, 128:] = jnp.where(instead, start, swapped[1 + v, rows, 128:])


def finish_kernel(pieces, out):
    core = lax.axis_index("sp") % 2
    inverse = [1.0 / spread(x) for x in range(4)]

    def total(odd, which, side, base, lanes, weight_lanes):
        value = None
        for x in range(4):
            slot = base + (2 * which + side - x) % 4
            term = pieces[4 * odd + x, slot, :, lanes].astype(F32) * inverse[x][:, weight_lanes]
            value = term if value is None else value + term
        return value

    value = None
    for x in range(4):
        term = pieces[x, 0].astype(F32) * inverse[x]
        value = term if value is None else value + term
    out[0] = value
    for m in range(1, 5):
        which, part = (m - 1) % 2, (m - 1) // 2
        lanes = slice(128 * part, 128 * part + 128)
        for side in range(2):
            place = slice(128 * side, 128 * side + 128)
            out[4 * m, :, place] = total(0, which, side, 1, lanes, lanes)
            out[4 * m - 2, :, place] = total(1, which, side, 1, lanes, lanes)
            out[4 * m - 1 - 2 * core, :, place] = total(1, which, side, 5, lanes, lanes)
            if m < 4:
                out[4 * m + 1 - 2 * core, :, place] = total(0, which, side, 5, lanes, lanes)
            else:

                @pl.when(core == 0)
                def _(which=which, side=side, lanes=lanes, place=place):
                    out[1, :, place] = total(0, which, side, 5, lanes, place)

                @pl.when(core == 1)
                def _(which=which, side=side, lanes=lanes, place=place):
                    out[15, :, place] = total(0, which, side, 5, lanes, lanes)


def vmem_spec():
    return pl.BlockSpec(memory_space=pltpu.VMEM)


def shape(*dims, dtype=BF16):
    return jax.ShapeDtypeStruct(dims, dtype)


def call(body, out_shape, n_in, flops, bytes_accessed, scratch=()):
    many = isinstance(out_shape, (tuple, list))
    return pl.pallas_call(
        body,
        out_shape=out_shape,
        in_specs=[vmem_spec() for _ in range(n_in)],
        out_specs=[vmem_spec() for _ in out_shape] if many else vmem_spec(),
        scratch_shapes=scratch,
        compiler_params=pltpu.CompilerParams(vmem_limit_bytes=VMEM_LIMIT),
        cost_estimate=pl.CostEstimate(flops=flops, bytes_accessed=bytes_accessed, transcendentals=0),
    )


def on_device(descriptors, sparse_points):
    barrier = lax.optimization_barrier

    def rows(body, envs, sums, n_in, *args):
        return call(body, (shape(envs, 512), shape(512, envs)) + sums, n_in, envs * 786432, envs << 12)(*args)

    gram_shape = shape(512, 256, dtype=F32)

    sib_points = fetch(sparse_points, other_core)
    piece = call(piece_kernel, shape(128, 512), 1, 0, 1 << 18)(sparse_points)
    first, second = fetch(piece, column(1)), fetch(piece, column(3))
    low, high = call(
        slice_kernel, (shape(FIRST, 512), shape(1024 - FIRST, 512)), 1, 0, 1 << 21
    )(descriptors)
    near = fetch(low, y_partner)
    env_a, rows_a, gram, points_hat = rows(
        own_kernel, 2048, (gram_shape, shape(512, 512)), 3, descriptors, sparse_points, sib_points
    )
    first, second, near, high, env_a, rows_a, gram, points_hat = barrier(
        (first, second, near, high, env_a, rows_a, gram, points_hat)
    )

    near_b = fetch(high, y_partner)
    quarter = call(quarter_kernel, shape(256, 512), 2, 1 << 20, 1 << 19)(first, second)
    quarters = [quarter] + [fetch(quarter, along_x(step)) for step in range(1, 4)]
    env_b, rows_b, gram = rows(more_kernel, 2 * FIRST, (gram_shape,), 4, near, fetch(near, other_core), points_hat, gram)
    grams = [gram]
    for v, points in enumerate(quarters):
        if v == 2:
            near_b, points, grams[1], grams[2] = barrier((near_b, points, grams[1], grams[2]))
            quarters[2] = points
        grams.append(
            call(column_kernel, gram_shape, 5, (2048 + 2 * FIRST) << 19, 1 << 23, (pltpu.VMEM((256, 2048 + 2 * FIRST), BF16),))(
                points, env_a, env_b, rows_a, rows_b
            )
        )
    rest = 2048 - 2 * FIRST
    scratch = (pltpu.VMEM((rest, 512), BF16), pltpu.VMEM((512, rest), BF16), pltpu.VMEM((256, rest), BF16))
    own, sib = call(last_kernel, (shape(5, 256, 256), shape(5, 256, 256)), 12, 2 * 1744830464, 1 << 23, scratch)(
        near_b, fetch(near_b, other_core), points_hat, *grams, *quarters
    )

    packed = call(pack_kernel, shape(8, 9, 32, 256), 2, 0, 1 << 21)(own, fetch(sib, other_core))
    pieces = lax.all_to_all(packed, "env", 0, 0, tiled=True)
    return call(finish_kernel, shape(17, 32, 256, dtype=F32), 1, 0, 1 << 21)(pieces)[None]


def solution(mesh):
    placed = (P("env", None), P("sp", None))
    return jax.shard_map(
        on_device, mesh=mesh, in_specs=placed, out_specs=P("sp", None, "env", None), check_vma=False
    )
```

```python
import functools

import jax
import jax.numpy as jnp
from jax import lax
from jax.experimental import pallas as pl
from jax.experimental.pallas import tpu as pltpu
from jax.sharding import PartitionSpec as P


F32, BF16 = jnp.float32, jnp.bfloat16
NT = (((1,), (1,)), ((), ()))
VMEM_LIMIT = 20 * 1024 * 1024


def split_index(i):
    env, sp = divmod(i, 32)
    y_hi, x = divmod(env, 4)
    q, core = divmod(sp, 2)
    z, y_lo = divmod(q, 2)
    return y_hi, x, z, y_lo, core


def join_index(y_hi, x, z, y_lo, core):
    return ((y_hi % 2) * 4 + x % 4) * 32 + ((z % 8) * 2 + y_lo % 2) * 2 + core % 2


def fetch(value, source_of):
    pairs = [(join_index(*source_of(*split_index(i))), i) for i in range(256)]
    return lax.ppermute(value, ("env", "sp"), pairs)


def other_core(y_hi, x, z, y_lo, core):
    return y_hi, x, z, y_lo, 1 - core


def near_x(y_hi, x, z, y_lo, core):
    return y_hi, x + 1 - 2 * core, z, y_lo, core


def next_z(y_hi, x, z, y_lo, core):
    return y_hi, x, z + 1, y_lo, core


def first_column(y_hi, x, z, y_lo, core):
    if x % 2 == 0:
        return y_hi, x, z + 1, y_lo, core
    y = (y_hi * 2 + y_lo + 1 - 2 * core) % 4
    return y // 2, x, z + y_lo, y % 2, core


def unit(values):
    values = values.astype(F32)
    total = jnp.sum(values * values, axis=1, keepdims=True)
    return (values * lax.rsqrt(total + 1e-06)).astype(BF16)


def fourth(products):
    squares = products * products
    return (squares * squares).astype(BF16)


def dot(a, b):
    return lax.dot_general(a, b, NT, preferred_element_type=F32)


CHUNK = 512


def weight_row():
    env = lax.axis_index("env")
    group = (env // 4) * 2 + (env % 4) // 2
    lanes = lax.broadcasted_iota(jnp.int32, (1, 256), 1)
    return (1.0 + ((lanes + 64 * group) % 256).astype(F32) / 256.0) * (16.0 / 16384.0)


def source_weight(e):
    group = (e // 4) * 2 + (e % 4) // 2
    lanes = lax.broadcasted_iota(jnp.int32, (1, 256), 1)
    return 1.0 / (1.0 + ((lanes + 64 * group) % 256).astype(F32) / 256.0)


def rows_of(points, raw, env_hat, rows_k):
    place = 0
    for ref in raw:
        for start in range(0, ref.shape[0], CHUNK):
            env = unit(ref[start:start + CHUNK, :])
            env_hat[place:place + CHUNK, :] = env
            rows_k[:, place:place + CHUNK] = fourth(dot(points, env))
            place += CHUNK


def slice_kernel(descriptors, first_out, second_out):
    half = pl.multiple_of((lax.axis_index("sp") % 2) * 1024, 1024)
    first_out[...] = descriptors[pl.ds(half, 512), :]
    second_out[...] = descriptors[pl.ds(half + 512, 512), :]


def own_kernel(own_env, own_points, sib_points, env_hat, rows_k, gram, points_hat):
    points_hat[:256, :] = unit(own_points[...])
    points_hat[256:, :] = unit(sib_points[...])
    rows_of(points_hat[...], (own_env,), env_hat, rows_k)
    gram[...] = dot(rows_k[...], rows_k[:256, :])


def more_kernel(near, far, points_hat, gram, env_hat, rows_k, gram_out):
    rows_of(points_hat[...], (near, far), env_hat, rows_k)
    gram_out[...] = gram[...] + dot(rows_k[...], rows_k[:256, :])


def last_kernel(near, far, points_hat, gram, env_hat, rows_k, own_out, sib_out):
    rows_of(points_hat[...], (near, far), env_hat, rows_k)
    total = ((gram[...] + dot(rows_k[...], rows_k[:256, :])) * weight_row()).astype(BF16)
    own_out[...] = total[:256]
    sib_out[...] = total[256:]


def column_kernel(points, *refs):
    envs, rows, own_out, sib_out, kept = refs[:3], refs[3:6], refs[6], refs[7], refs[8]
    point_hat = unit(points[...])
    total, place = None, 0
    for env in envs:
        for start in range(0, env.shape[0], CHUNK):
            kept[:, place:place + CHUNK] = fourth(dot(point_hat, env[start:start + CHUNK, :]))
            place += CHUNK
    place = 0
    for row in rows:
        term = dot(row[...], kept[:, place:place + row.shape[1]])
        total = term if total is None else total + term
        place += row.shape[1]
    total = (total * weight_row()).astype(BF16)
    own_out[...] = total[:256]
    sib_out[...] = total[256:]


def pack_kernel(*refs):
    own, swapped, out = refs[:5], refs[5:10], refs[10]
    even_x = lax.axis_index("env") % 2 == 0
    shift = jnp.logical_and(even_x, lax.axis_index("sp") % 2 == 0)
    for e in range(8):
        rows = slice(32 * e, 32 * e + 32)
        for m in range(5):
            out[e, m] = own[m][rows, :]
        for m in range(1, 5):
            out[e, 4 + m] = jnp.where(shift, swapped[m - 1][rows, :], swapped[m][rows, :])


def finish_kernel(pieces, out):
    core = lax.axis_index("sp") % 2

    def total(parity, slot):
        value = None
        for e in range(parity, 8, 2):
            term = pieces[e, slot].astype(F32) * source_weight(e)
            value = term if value is None else value + term
        return value

    out[0] = total(0, 0)
    for m in range(1, 5):
        out[4 * m] = total(0, m)
        out[4 * m - 2] = total(1, m)
        out[4 * m - 3 + 2 * core] = total(0, 4 + m)
        out[4 * m - 1 - 2 * core] = total(1, 4 + m)


def vmem_spec():
    return pl.BlockSpec(memory_space=pltpu.VMEM)


def shape(*dims, dtype=BF16):
    return jax.ShapeDtypeStruct(dims, dtype)


def call(body, out_shape, n_in, flops, bytes_accessed, scratch=()):
    many = isinstance(out_shape, (tuple, list))
    return pl.pallas_call(
        body,
        out_shape=out_shape,
        in_specs=[vmem_spec() for _ in range(n_in)],
        out_specs=[vmem_spec() for _ in out_shape] if many else vmem_spec(),
        scratch_shapes=scratch,
        compiler_params=pltpu.CompilerParams(vmem_limit_bytes=VMEM_LIMIT),
        cost_estimate=pl.CostEstimate(flops=flops, bytes_accessed=bytes_accessed, transcendentals=0),
    )


def on_device(descriptors, sparse_points):
    barrier = lax.optimization_barrier

    def rows(body, envs, sums, n_in, *args):
        return call(body, (shape(envs, 512), shape(512, envs)) + sums, n_in, envs * 786432, envs << 12)(*args)

    gram_shape = shape(512, 256, dtype=F32)
    pair = (shape(256, 256), shape(256, 256))

    column = fetch(sparse_points, first_column)
    sib_points = fetch(sparse_points, other_core)
    env_a, rows_a, gram, points_hat = rows(
        own_kernel, 2048, (gram_shape, shape(512, 512)), 3, descriptors, sparse_points, sib_points
    )
    columns = [column]
    column, later, env_a, rows_a, gram, points_hat = barrier(
        (column, descriptors, env_a, rows_a, gram, points_hat)
    )

    columns.append(fetch(column, next_z))
    low, high = call(slice_kernel, (shape(512, 512), shape(512, 512)), 1, 0, 1 << 21)(later)
    near, high, column = barrier((fetch(low, near_x), high, columns[1]))

    columns.append(fetch(column, next_z))
    near_b = fetch(high, near_x)
    far = fetch(near, other_core)
    env_b, rows_b, gram = rows(more_kernel, 1024, (gram_shape,), 4, near, far, points_hat, gram)
    near_b, column, env_b, rows_b, gram = barrier((near_b, columns[2], env_b, rows_b, gram))

    columns.append(fetch(column, next_z))
    env_c, rows_c, own, sib = rows(
        last_kernel, 1024, pair, 4, near_b, fetch(near_b, other_core), points_hat, gram
    )
    owns, sibs = [own], [sib]

    def take(points):
        own, sib = call(
            column_kernel, pair, 7, 2 * 1073741824, 1 << 23, (pltpu.VMEM((256, 4096), BF16),)
        )(points, env_a, env_b, env_c, rows_a, rows_b, rows_c)
        owns.append(own)
        sibs.append(sib)

    for points in columns[:3]:
        take(points)
    column, *owns = barrier((columns[3], *owns))
    take(column)

    swapped = [fetch(sib, other_core) for sib in sibs]
    packed = call(pack_kernel, shape(8, 9, 32, 256), 10, 0, 1 << 21)(*owns, *swapped)
    pieces = lax.all_to_all(packed, "env", 0, 0, tiled=True)
    return call(finish_kernel, shape(17, 32, 256, dtype=F32), 1, 0, 1 << 21)(pieces)[None]


def solution(mesh):
    placed = (P("env", None), P("sp", None))
    return jax.shard_map(
        on_device, mesh=mesh, in_specs=placed, out_specs=P("sp", None, "env", None), check_vma=False
    )
```

```python
import functools

import jax
import jax.numpy as jnp
from jax import lax
from jax.experimental import pallas as pl
from jax.experimental.pallas import tpu as pltpu
from jax.sharding import PartitionSpec as P


F32, BF16 = jnp.float32, jnp.bfloat16
NT = (((1,), (1,)), ((), ()))
VMEM_LIMIT = 20 * 1024 * 1024


def split_index(i):
    env, sp = divmod(i, 32)
    y_hi, x = divmod(env, 4)
    q, core = divmod(sp, 2)
    z, y_lo = divmod(q, 2)
    return y_hi, x, z, y_lo, core


def join_index(y_hi, x, z, y_lo, core):
    return ((y_hi % 2) * 4 + x % 4) * 32 + ((z % 8) * 2 + y_lo % 2) * 2 + core % 2


def fetch(value, source_of):
    pairs = [(join_index(*source_of(*split_index(i))), i) for i in range(256)]
    return lax.ppermute(value, ("env", "sp"), pairs)


def other_core(y_hi, x, z, y_lo, core):
    return y_hi, x, z, y_lo, 1 - core


def near_x(y_hi, x, z, y_lo, core):
    return y_hi, x + 1 - 2 * core, z, y_lo, core


def next_z(y_hi, x, z, y_lo, core):
    return y_hi, x, z + 1, y_lo, core


def first_column(y_hi, x, z, y_lo, core):
    if x % 2 == 0:
        return y_hi, x, z + 1, y_lo, core
    y = (y_hi * 2 + y_lo + 1 - 2 * core) % 4
    return y // 2, x, z + y_lo, y % 2, core


def unit(values):
    values = values.astype(F32)
    total = jnp.sum(values * values, axis=1, keepdims=True)
    return (values * lax.rsqrt(total + 1e-06)).astype(BF16)


def fourth(products):
    squares = products * products
    return (squares * squares).astype(BF16)


def dot(a, b):
    return lax.dot_general(a, b, NT, preferred_element_type=F32)


CHUNK = 512


def weight_row():
    env = lax.axis_index("env")
    group = (env // 4) * 2 + (env % 4) // 2
    lanes = lax.broadcasted_iota(jnp.int32, (1, 256), 1)
    return (1.0 + ((lanes + 64 * group) % 256).astype(F32) / 256.0) * (16.0 / 16384.0)


def source_weight(e):
    group = (e // 4) * 2 + (e % 4) // 2
    lanes = lax.broadcasted_iota(jnp.int32, (1, 256), 1)
    return 1.0 / (1.0 + ((lanes + 64 * group) % 256).astype(F32) / 256.0)


def rows_of(points, raw, env_hat, rows_k):
    place = 0
    for ref in raw:
        for start in range(0, ref.shape[0], CHUNK):
            env = unit(ref[start:start + CHUNK, :])
            env_hat[place:place + CHUNK, :] = env
            rows_k[:, place:place + CHUNK] = fourth(dot(points, env))
            place += CHUNK


def slice_kernel(descriptors, first_out, second_out):
    half = pl.multiple_of((lax.axis_index("sp") % 2) * 1024, 1024)
    first_out[...] = descriptors[pl.ds(half, 512), :]
    second_out[...] = descriptors[pl.ds(half + 512, 512), :]


def own_kernel(own_env, own_points, sib_points, env_hat, rows_k, gram, points_hat):
    points_hat[:256, :] = unit(own_points[...])
    points_hat[256:, :] = unit(sib_points[...])
    rows_of(points_hat[...], (own_env,), env_hat, rows_k)
    gram[...] = dot(rows_k[...], rows_k[:256, :])


def more_kernel(near, far, points_hat, gram, env_hat, rows_k, gram_out):
    rows_of(points_hat[...], (near, far), env_hat, rows_k)
    gram_out[...] = gram[...] + dot(rows_k[...], rows_k[:256, :])


def kernel_values(point_hat, envs, kept):
    place = 0
    for env in envs:
        for start in range(0, env.shape[0], CHUNK):
            kept[:, place:place + CHUNK] = fourth(dot(point_hat, env[start:start + CHUNK, :]))
            place += CHUNK


def products(rows, kept):
    total, place = None, 0
    for row in rows:
        term = dot(row[...], kept[:, place:place + row.shape[1]])
        total = term if total is None else total + term
        place += row.shape[1]
    return total


def give(gram, own_out, sib_out):
    total = (gram * weight_row()).astype(BF16)
    own_out[...] = total[:256]
    sib_out[...] = total[256:]


def begin_kernel(points, env_a, env_b, rows_a, rows_b, point_hat, gram, kept):
    point_hat[...] = unit(points[...])
    kernel_values(point_hat[...], (env_a, env_b), kept)
    gram[...] = products((rows_a, rows_b), kept)


def last_kernel(near, far, points_hat, gram, first_hat, first_gram, second_hat, second_gram,
                env_hat, rows_k, own0, sib0, own1, sib1, own2, sib2, kept):
    rows_of(points_hat[...], (near, far), env_hat, rows_k)
    give(gram[...] + dot(rows_k[...], rows_k[:256, :]), own0, sib0)
    for point_hat, begun, own, sib in ((first_hat, first_gram, own1, sib1), (second_hat, second_gram, own2, sib2)):
        kernel_values(point_hat[...], (env_hat,), kept)
        give(begun[...] + products((rows_k,), kept), own, sib)


def column_kernel(points, *refs):
    kernel_values(unit(points[...]), refs[:3], refs[8])
    give(products(refs[3:6], refs[8]), refs[6], refs[7])


def pack_kernel(*refs):
    own, swapped, out = refs[:5], refs[5:10], refs[10]
    even_x = lax.axis_index("env") % 2 == 0
    shift = jnp.logical_and(even_x, lax.axis_index("sp") % 2 == 0)
    for e in range(8):
        rows = slice(32 * e, 32 * e + 32)
        for m in range(5):
            out[e, m] = own[m][rows, :]
        for m in range(1, 5):
            out[e, 4 + m] = jnp.where(shift, swapped[m - 1][rows, :], swapped[m][rows, :])


def finish_kernel(pieces, out):
    core = lax.axis_index("sp") % 2

    def total(parity, slot):
        value = None
        for e in range(parity, 8, 2):
            term = pieces[e, slot].astype(F32) * source_weight(e)
            value = term if value is None else value + term
        return value

    out[0] = total(0, 0)
    for m in range(1, 5):
        out[4 * m] = total(0, m)
        out[4 * m - 2] = total(1, m)
        out[4 * m - 3 + 2 * core] = total(0, 4 + m)
        out[4 * m - 1 - 2 * core] = total(1, 4 + m)


def vmem_spec():
    return pl.BlockSpec(memory_space=pltpu.VMEM)


def shape(*dims, dtype=BF16):
    return jax.ShapeDtypeStruct(dims, dtype)


def call(body, out_shape, n_in, flops, bytes_accessed, scratch=()):
    many = isinstance(out_shape, (tuple, list))
    return pl.pallas_call(
        body,
        out_shape=out_shape,
        in_specs=[vmem_spec() for _ in range(n_in)],
        out_specs=[vmem_spec() for _ in out_shape] if many else vmem_spec(),
        scratch_shapes=scratch,
        compiler_params=pltpu.CompilerParams(vmem_limit_bytes=VMEM_LIMIT),
        cost_estimate=pl.CostEstimate(flops=flops, bytes_accessed=bytes_accessed, transcendentals=0),
    )


def on_device(descriptors, sparse_points):
    barrier = lax.optimization_barrier

    def rows(body, envs, sums, n_in, *args):
        return call(body, (shape(envs, 512), shape(512, envs)) + sums, n_in, envs * 786432, envs << 12)(*args)

    gram_shape = shape(512, 256, dtype=F32)
    pair = (shape(256, 256), shape(256, 256))

    column = fetch(sparse_points, first_column)
    sib_points = fetch(sparse_points, other_core)
    env_a, rows_a, gram, points_hat = rows(
        own_kernel, 2048, (gram_shape, shape(512, 512)), 3, descriptors, sparse_points, sib_points
    )
    columns = [column]
    column, later, env_a, rows_a, gram, points_hat = barrier(
        (column, descriptors, env_a, rows_a, gram, points_hat)
    )

    columns.append(fetch(column, next_z))
    low, high = call(slice_kernel, (shape(512, 512), shape(512, 512)), 1, 0, 1 << 21)(later)
    near, high, column = barrier((fetch(low, near_x), high, columns[1]))

    columns.append(fetch(column, next_z))
    near_b = fetch(high, near_x)
    far = fetch(near, other_core)
    env_b, rows_b, gram = rows(more_kernel, 1024, (gram_shape,), 4, near, far, points_hat, gram)
    begun = []
    for points in columns[:2]:
        begun += call(
            begin_kernel, (shape(256, 512), gram_shape), 5, 2 * 805306368, 1 << 23, (pltpu.VMEM((256, 3072), BF16),)
        )(points, env_a, env_b, rows_a, rows_b)
    near_b, column, env_b, rows_b, gram, *begun = barrier((near_b, columns[2], env_b, rows_b, gram, *begun))

    last = fetch(column, next_z)
    env_c, rows_c, *sums = call(
        last_kernel, (shape(1024, 512), shape(512, 1024)) + 3 * pair, 8, 2 * 1207959552, 1 << 23,
        (pltpu.VMEM((256, 1024), BF16),)
    )(near_b, fetch(near_b, other_core), points_hat, gram, *begun)

    def take(points):
        return call(
            column_kernel, pair, 7, 2 * 1073741824, 1 << 23, (pltpu.VMEM((256, 4096), BF16),)
        )(points, env_a, env_b, env_c, rows_a, rows_b, rows_c)

    sums += take(column)
    owns, swapped = sums[0::2], [fetch(sib, other_core) for sib in sums[1::2]]
    last, *sums = barrier((last, *owns, *swapped))
    owns, swapped = sums[:4], sums[4:]

    own, sib = take(last)
    packed = call(pack_kernel, shape(8, 9, 32, 256), 10, 0, 1 << 21)(*owns, own, *swapped, fetch(sib, other_core))
    pieces = lax.all_to_all(packed, "env", 0, 0, tiled=True)
    return call(finish_kernel, shape(17, 32, 256, dtype=F32), 1, 0, 1 << 21)(pieces)[None]


def solution(mesh):
    placed = (P("env", None), P("sp", None))
    return jax.shard_map(
        on_device, mesh=mesh, in_specs=placed, out_specs=P("sp", None, "env", None), check_vma=False
    )
```

```python
import functools

import jax
import jax.numpy as jnp
from jax import lax
from jax.experimental import pallas as pl
from jax.experimental.pallas import tpu as pltpu
from jax.sharding import PartitionSpec as P


F32, BF16 = jnp.float32, jnp.bfloat16
NT = (((1,), (1,)), ((), ()))
VMEM_LIMIT = 20 * 1024 * 1024


def split_index(i):
    env, sp = divmod(i, 32)
    y_hi, x = divmod(env, 4)
    q, core = divmod(sp, 2)
    z, y_lo = divmod(q, 2)
    return y_hi, x, z, y_lo, core


def join_index(y_hi, x, z, y_lo, core):
    return ((y_hi % 2) * 4 + x % 4) * 32 + ((z % 8) * 2 + y_lo % 2) * 2 + core % 2


def fetch(value, source_of):
    pairs = [(join_index(*source_of(*split_index(i))), i) for i in range(256)]
    return lax.ppermute(value, ("env", "sp"), pairs)


def other_core(y_hi, x, z, y_lo, core):
    return y_hi, x, z, y_lo, 1 - core


def near_x(y_hi, x, z, y_lo, core):
    return y_hi, x + 1 - 2 * core, z, y_lo, core


def next_z(y_hi, x, z, y_lo, core):
    return y_hi, x, z + 1, y_lo, core


def first_column(y_hi, x, z, y_lo, core):
    if x % 2 == 0:
        return y_hi, x, z + 1, y_lo, core
    y = (y_hi * 2 + y_lo + 1 - 2 * core) % 4
    return y // 2, x, z + y_lo, y % 2, core


def unit(values):
    values = values.astype(F32)
    total = jnp.sum(values * values, axis=1, keepdims=True)
    return (values * lax.rsqrt(total + 1e-06)).astype(BF16)


def fourth(products):
    squares = products * products
    return (squares * squares).astype(BF16)


def dot(a, b):
    return lax.dot_general(a, b, NT, preferred_element_type=F32)


CHUNK = 512
PIECES = 4


def weight_row():
    env = lax.axis_index("env")
    group = (env // 4) * 2 + (env % 4) // 2
    lanes = lax.broadcasted_iota(jnp.int32, (1, 256), 1)
    return (1.0 + ((lanes + 64 * group) % 256).astype(F32) / 256.0) * (16.0 / 16384.0)


def source_weight(e):
    group = (e // 4) * 2 + (e % 4) // 2
    lanes = lax.broadcasted_iota(jnp.int32, (1, 256), 1)
    return 1.0 / (1.0 + ((lanes + 64 * group) % 256).astype(F32) / 256.0)


def rows_of(points, raw, env_hat, rows_k):
    place = 0
    for ref in raw:
        for start in range(0, ref.shape[0], CHUNK):
            size = min(CHUNK, ref.shape[0] - start)
            env = unit(ref[start:start + size, :])
            env_hat[place:place + size, :] = env
            rows_k[:, place:place + size] = fourth(dot(points, env))
            place += size


def slice_kernel(descriptors, out):
    half = pl.multiple_of((lax.axis_index("sp") % 2) * 1024, 1024)
    out[...] = descriptors[pl.ds(half, 1024), :]


def split_kernel(near, *outs):
    size = near.shape[0] // len(outs)
    for i, out in enumerate(outs):
        out[...] = near[size * i:size * i + size, :]


def own_kernel(own_env, own_points, sib_points, env_hat, rows_k, gram, points_hat):
    points_hat[:256, :] = unit(own_points[...])
    points_hat[256:, :] = unit(sib_points[...])
    rows_of(points_hat[...], (own_env,), env_hat, rows_k)
    gram[...] = dot(rows_k[...], rows_k[:256, :])


def kernel_values(point_hat, envs, kept):
    place = 0
    for env in envs:
        for start in range(0, env.shape[0], CHUNK):
            kept[:, place:place + CHUNK] = fourth(dot(point_hat, env[start:start + CHUNK, :]))
            place += CHUNK


def products(rows, kept):
    total, place = None, 0
    for row in rows:
        term = dot(row[...], kept[:, place:place + row.shape[1]])
        total = term if total is None else total + term
        place += row.shape[1]
    return total


def give(gram, own_out, sib_out):
    total = (gram * weight_row()).astype(BF16)
    own_out[...] = total[:256]
    sib_out[...] = total[256:]


def more_kernel(*refs):
    points_hat, gram, env_hat, rows_k, own_out, sib_out = refs[2 * PIECES:]
    rows_of(points_hat[...], refs[:2 * PIECES], env_hat, rows_k)
    give(gram[...] + dot(rows_k[...], rows_k[:256, :]), own_out, sib_out)


def column_kernel(points, *refs):
    kernel_values(unit(points[...]), refs[:2], refs[6])
    give(products(refs[2:4], refs[6]), refs[4], refs[5])


def pack_kernel(*refs):
    own, swapped, out = refs[:5], refs[5:10], refs[10]
    even_x = lax.axis_index("env") % 2 == 0
    shift = jnp.logical_and(even_x, lax.axis_index("sp") % 2 == 0)
    for e in range(8):
        rows = slice(32 * e, 32 * e + 32)
        for m in range(5):
            out[e, m] = own[m][rows, :]
        for m in range(1, 5):
            out[e, 4 + m] = jnp.where(shift, swapped[m - 1][rows, :], swapped[m][rows, :])


def finish_kernel(pieces, out):
    core = lax.axis_index("sp") % 2

    def total(parity, slot):
        value = None
        for e in range(parity, 8, 2):
            term = pieces[e, slot].astype(F32) * source_weight(e)
            value = term if value is None else value + term
        return value

    out[0] = total(0, 0)
    for m in range(1, 5):
        out[4 * m] = total(0, m)
        out[4 * m - 2] = total(1, m)
        out[4 * m - 3 + 2 * core] = total(0, 4 + m)
        out[4 * m - 1 - 2 * core] = total(1, 4 + m)


def vmem_spec():
    return pl.BlockSpec(memory_space=pltpu.VMEM)


def shape(*dims, dtype=BF16):
    return jax.ShapeDtypeStruct(dims, dtype)


def call(body, out_shape, n_in, flops, bytes_accessed, scratch=()):
    many = isinstance(out_shape, (tuple, list))
    return pl.pallas_call(
        body,
        out_shape=out_shape,
        in_specs=[vmem_spec() for _ in range(n_in)],
        out_specs=[vmem_spec() for _ in out_shape] if many else vmem_spec(),
        scratch_shapes=scratch,
        compiler_params=pltpu.CompilerParams(vmem_limit_bytes=VMEM_LIMIT),
        cost_estimate=pl.CostEstimate(flops=flops, bytes_accessed=bytes_accessed, transcendentals=0),
    )


def on_device(descriptors, sparse_points):
    barrier = lax.optimization_barrier

    def rows(body, envs, sums, n_in, *args):
        return call(body, (shape(envs, 512), shape(512, envs)) + sums, n_in, envs * 786432, envs << 12)(*args)

    gram_shape = shape(512, 256, dtype=F32)
    pair = (shape(256, 256), shape(256, 256))

    column = fetch(sparse_points, first_column)
    sib_points = fetch(sparse_points, other_core)
    env_a, rows_a, gram, points_hat = rows(
        own_kernel, 2048, (gram_shape, shape(512, 512)), 3, descriptors, sparse_points, sib_points
    )
    columns = [column]
    column, later, env_a, rows_a, gram, points_hat = barrier(
        (column, descriptors, env_a, rows_a, gram, points_hat)
    )

    columns.append(fetch(column, next_z))
    near = fetch(call(slice_kernel, shape(1024, 512), 1, 0, 1 << 21)(later), near_x)
    near, _ = barrier((near, columns[1]))

    columns.append(fetch(columns[1], next_z))
    near = call(split_kernel, PIECES * (shape(1024 // PIECES, 512),), 1, 0, 1 << 21)(near)
    far = [fetch(piece, other_core) for piece in near]
    env_b, rows_b, own, sib = rows(more_kernel, 2048, pair, 2 * PIECES + 2, *near, *far, points_hat, gram)

    def take(points):
        return call(
            column_kernel, pair, 5, 2 * 1073741824, 1 << 23, (pltpu.VMEM((256, 4096), BF16),)
        )(points, env_a, env_b, rows_a, rows_b)

    sums = [own, sib]
    column = columns[2]

    last = fetch(column, next_z)
    for points in columns[:3]:
        sums += take(points)
    owns, swapped = sums[0::2], [fetch(sib, other_core) for sib in sums[1::2]]
    last, *sums = barrier((last, *owns, *swapped))
    owns, swapped = sums[:4], sums[4:]

    own, sib = take(last)
    packed = call(pack_kernel, shape(8, 9, 32, 256), 10, 0, 1 << 21)(*owns, own, *swapped, fetch(sib, other_core))
    pieces = lax.all_to_all(packed, "env", 0, 0, tiled=True)
    return call(finish_kernel, shape(17, 32, 256, dtype=F32), 1, 0, 1 << 21)(pieces)[None]


def solution(mesh):
    placed = (P("env", None), P("sp", None))
    return jax.shard_map(
        on_device, mesh=mesh, in_specs=placed, out_specs=P("sp", None, "env", None), check_vma=False
    )
```

```python
import functools

import jax
import jax.numpy as jnp
from jax import lax
from jax.experimental import pallas as pl
from jax.experimental.pallas import tpu as pltpu
from jax.sharding import PartitionSpec as P


F32, BF16 = jnp.float32, jnp.bfloat16
NT = (((1,), (1,)), ((), ()))
VMEM_LIMIT = 20 * 1024 * 1024


def split_index(i):
    env, sp = divmod(i, 32)
    y_hi, x = divmod(env, 4)
    q, core = divmod(sp, 2)
    z, y_lo = divmod(q, 2)
    return y_hi, x, z, y_lo, core


def join_index(y_hi, x, z, y_lo, core):
    return ((y_hi % 2) * 4 + x % 4) * 32 + ((z % 8) * 2 + y_lo % 2) * 2 + core % 2


def fetch(value, source_of):
    pairs = [(join_index(*source_of(*split_index(i))), i) for i in range(256)]
    return lax.ppermute(value, ("env", "sp"), pairs)


def other_core(y_hi, x, z, y_lo, core):
    return y_hi, x, z, y_lo, 1 - core


def near_x(y_hi, x, z, y_lo, core):
    return y_hi, x + 1 - 2 * core, z, y_lo, core


def next_z(y_hi, x, z, y_lo, core):
    return y_hi, x, z + 1, y_lo, core


def first_column(y_hi, x, z, y_lo, core):
    if x % 2 == 0:
        return y_hi, x, z + 1, y_lo, core
    y = (y_hi * 2 + y_lo + 1 - 2 * core) % 4
    return y // 2, x, z + y_lo, y % 2, core


def unit(values):
    values = values.astype(F32)
    total = jnp.sum(values * values, axis=1, keepdims=True)
    return (values * lax.rsqrt(total + 1e-06)).astype(BF16)


def fourth(products):
    squares = products * products
    return (squares * squares).astype(BF16)


def dot(a, b):
    return lax.dot_general(a, b, NT, preferred_element_type=F32)


CHUNK = 512
PIECES = 4


def weight_row():
    env = lax.axis_index("env")
    group = (env // 4) * 2 + (env % 4) // 2
    lanes = lax.broadcasted_iota(jnp.int32, (1, 256), 1)
    return (1.0 + ((lanes + 64 * group) % 256).astype(F32) / 256.0) * (16.0 / 16384.0)


def source_weight(e):
    group = (e // 4) * 2 + (e % 4) // 2
    lanes = lax.broadcasted_iota(jnp.int32, (1, 256), 1)
    return 1.0 / (1.0 + ((lanes + 64 * group) % 256).astype(F32) / 256.0)


def rows_of(points, raw, env_hat, rows_k):
    place = 0
    for ref in raw:
        for start in range(0, ref.shape[0], CHUNK):
            size = min(CHUNK, ref.shape[0] - start)
            env = unit(ref[start:start + size, :])
            env_hat[place:place + size, :] = env
            rows_k[:, place:place + size] = fourth(dot(points, env))
            place += size


def slice_kernel(descriptors, out):
    half = pl.multiple_of((lax.axis_index("sp") % 2) * 1024, 1024)
    out[...] = descriptors[pl.ds(half, 1024), :]


def split_kernel(near, *outs):
    size = near.shape[0] // len(outs)
    for i, out in enumerate(outs):
        out[...] = near[size * i:size * i + size, :]


def own_kernel(own_env, own_points, sib_points, env_hat, rows_k, gram, points_hat):
    points_hat[:256, :] = unit(own_points[...])
    points_hat[256:, :] = unit(sib_points[...])
    rows_of(points_hat[...], (own_env,), env_hat, rows_k)
    gram[...] = dot(rows_k[...], rows_k[:256, :])


def kernel_values(point_hat, envs, kept):
    place = 0
    for env in envs:
        for start in range(0, env.shape[0], CHUNK):
            kept[:, place:place + CHUNK] = fourth(dot(point_hat, env[start:start + CHUNK, :]))
            place += CHUNK


def products(rows, kept):
    total, place = None, 0
    for row in rows:
        term = dot(row[...], kept[:, place:place + row.shape[1]])
        total = term if total is None else total + term
        place += row.shape[1]
    return total


def give(gram, own_out, sib_out):
    total = (gram * weight_row()).astype(BF16)
    own_out[...] = total[:256]
    sib_out[...] = total[256:]


def begin_kernel(points, env_a, rows_a, point_hat, gram, kept):
    point_hat[...] = unit(points[...])
    kernel_values(point_hat[...], (env_a,), kept)
    gram[...] = products((rows_a,), kept)


def more_kernel(*refs):
    points_hat, gram, first_hat, first_gram, second_hat, second_gram = refs[2 * PIECES:2 * PIECES + 6]
    env_hat, rows_k, own0, sib0, own1, sib1, own2, sib2, kept = refs[2 * PIECES + 6:]
    rows_of(points_hat[...], refs[:2 * PIECES], env_hat, rows_k)
    give(gram[...] + dot(rows_k[...], rows_k[:256, :]), own0, sib0)
    for point_hat, begun, own, sib in ((first_hat, first_gram, own1, sib1), (second_hat, second_gram, own2, sib2)):
        kernel_values(point_hat[...], (env_hat,), kept)
        give(begun[...] + products((rows_k,), kept), own, sib)


def column_kernel(points, *refs):
    kernel_values(unit(points[...]), refs[:2], refs[6])
    give(products(refs[2:4], refs[6]), refs[4], refs[5])


def pack_kernel(*refs):
    own, swapped, out = refs[:5], refs[5:10], refs[10]
    even_x = lax.axis_index("env") % 2 == 0
    shift = jnp.logical_and(even_x, lax.axis_index("sp") % 2 == 0)
    for e in range(8):
        rows = slice(32 * e, 32 * e + 32)
        for m in range(5):
            out[e, m] = own[m][rows, :]
        for m in range(1, 5):
            out[e, 4 + m] = jnp.where(shift, swapped[m - 1][rows, :], swapped[m][rows, :])


def finish_kernel(pieces, out):
    core = lax.axis_index("sp") % 2

    def total(parity, slot):
        value = None
        for e in range(parity, 8, 2):
            term = pieces[e, slot].astype(F32) * source_weight(e)
            value = term if value is None else value + term
        return value

    out[0] = total(0, 0)
    for m in range(1, 5):
        out[4 * m] = total(0, m)
        out[4 * m - 2] = total(1, m)
        out[4 * m - 3 + 2 * core] = total(0, 4 + m)
        out[4 * m - 1 - 2 * core] = total(1, 4 + m)


def vmem_spec():
    return pl.BlockSpec(memory_space=pltpu.VMEM)


def shape(*dims, dtype=BF16):
    return jax.ShapeDtypeStruct(dims, dtype)


def call(body, out_shape, n_in, flops, bytes_accessed, scratch=()):
    many = isinstance(out_shape, (tuple, list))
    return pl.pallas_call(
        body,
        out_shape=out_shape,
        in_specs=[vmem_spec() for _ in range(n_in)],
        out_specs=[vmem_spec() for _ in out_shape] if many else vmem_spec(),
        scratch_shapes=scratch,
        compiler_params=pltpu.CompilerParams(vmem_limit_bytes=VMEM_LIMIT),
        cost_estimate=pl.CostEstimate(flops=flops, bytes_accessed=bytes_accessed, transcendentals=0),
    )


def on_device(descriptors, sparse_points):
    barrier = lax.optimization_barrier

    def rows(body, envs, sums, n_in, *args):
        return call(body, (shape(envs, 512), shape(512, envs)) + sums, n_in, envs * 786432, envs << 12)(*args)

    gram_shape = shape(512, 256, dtype=F32)
    pair = (shape(256, 256), shape(256, 256))

    column = fetch(sparse_points, first_column)
    sib_points = fetch(sparse_points, other_core)
    env_a, rows_a, gram, points_hat = rows(
        own_kernel, 2048, (gram_shape, shape(512, 512)), 3, descriptors, sparse_points, sib_points
    )
    columns = [column]
    column, later, env_a, rows_a, gram, points_hat = barrier(
        (column, descriptors, env_a, rows_a, gram, points_hat)
    )

    kept = (pltpu.VMEM((256, 2048), BF16),)

    def begin(points):
        return call(begin_kernel, (shape(256, 512), gram_shape), 3, 1 << 30, 1 << 22, kept)(points, env_a, rows_a)

    columns.append(fetch(column, next_z))
    near = fetch(call(slice_kernel, shape(1024, 512), 1, 0, 1 << 21)(later), near_x)
    column, *begun = barrier((columns[1], *begin(columns[0])))

    columns.append(fetch(column, next_z))
    near, *others = barrier((near, *begin(column)))
    begun += others
    near = call(split_kernel, PIECES * (shape(1024 // PIECES, 512),), 1, 0, 1 << 21)(near)
    far = [fetch(piece, other_core) for piece in near]

    last = fetch(columns[2], next_z)
    env_b, rows_b, *sums = call(
        more_kernel, (shape(2048, 512), shape(512, 2048)) + 3 * pair, 2 * PIECES + 6, 7 << 29, 1 << 23, kept
    )(*near, *far, points_hat, gram, *begun)

    def take(points):
        return call(
            column_kernel, pair, 5, 2 * 1073741824, 1 << 23, (pltpu.VMEM((256, 4096), BF16),)
        )(points, env_a, env_b, rows_a, rows_b)

    sums += take(columns[2])
    owns, swapped = sums[0::2], [fetch(sib, other_core) for sib in sums[1::2]]
    last, *sums = barrier((last, *owns, *swapped))
    owns, swapped = sums[:4], sums[4:]

    own, sib = take(last)
    packed = call(pack_kernel, shape(8, 9, 32, 256), 10, 0, 1 << 21)(*owns, own, *swapped, fetch(sib, other_core))
    pieces = lax.all_to_all(packed, "env", 0, 0, tiled=True)
    return call(finish_kernel, shape(17, 32, 256, dtype=F32), 1, 0, 1 << 21)(pieces)[None]


def solution(mesh):
    placed = (P("env", None), P("sp", None))
    return jax.shard_map(
        on_device, mesh=mesh, in_specs=placed, out_specs=P("sp", None, "env", None), check_vma=False
    )
```

```python
import functools

import jax
import jax.numpy as jnp
from jax import lax
from jax.experimental import pallas as pl
from jax.experimental.pallas import tpu as pltpu
from jax.sharding import PartitionSpec as P


F32, BF16 = jnp.float32, jnp.bfloat16
NT = (((1,), (1,)), ((), ()))
VMEM_LIMIT = 20 * 1024 * 1024


def split_index(i):
    env, sp = divmod(i, 32)
    y_hi, x = divmod(env, 4)
    q, core = divmod(sp, 2)
    z, y_lo = divmod(q, 2)
    return y_hi, x, z, y_lo, core


def join_index(y_hi, x, z, y_lo, core):
    return ((y_hi % 2) * 4 + x % 4) * 32 + ((z % 8) * 2 + y_lo % 2) * 2 + core % 2


def fetch(value, source_of):
    pairs = [(join_index(*source_of(*split_index(i))), i) for i in range(256)]
    return lax.ppermute(value, ("env", "sp"), pairs)


def other_core(y_hi, x, z, y_lo, core):
    return y_hi, x, z, y_lo, 1 - core


def near_x(y_hi, x, z, y_lo, core):
    return y_hi, x + 1 - 2 * core, z, y_lo, core


def next_z(y_hi, x, z, y_lo, core):
    return y_hi, x, z + 1, y_lo, core


def first_column(y_hi, x, z, y_lo, core):
    if x % 2 == 0:
        return y_hi, x, z + 1, y_lo, core
    y = (y_hi * 2 + y_lo + 1 - 2 * core) % 4
    return y // 2, x, z + y_lo, y % 2, core


def unit(values):
    values = values.astype(F32)
    total = jnp.sum(values * values, axis=1, keepdims=True)
    return (values * lax.rsqrt(total + 1e-06)).astype(BF16)


def fourth(products):
    squares = products * products
    return (squares * squares).astype(BF16)


def dot(a, b):
    return lax.dot_general(a, b, NT, preferred_element_type=F32)


CHUNK = 512
PIECES = 4


def weight_row():
    env = lax.axis_index("env")
    group = (env // 4) * 2 + (env % 4) // 2
    lanes = lax.broadcasted_iota(jnp.int32, (1, 256), 1)
    return (1.0 + ((lanes + 64 * group) % 256).astype(F32) / 256.0) * (16.0 / 16384.0)


def source_weight(e):
    group = (e // 4) * 2 + (e % 4) // 2
    lanes = lax.broadcasted_iota(jnp.int32, (1, 256), 1)
    return 1.0 / (1.0 + ((lanes + 64 * group) % 256).astype(F32) / 256.0)


def rows_of(points, raw, env_hat, rows_k):
    place = 0
    for ref in raw:
        for start in range(0, ref.shape[0], CHUNK):
            size = min(CHUNK, ref.shape[0] - start)
            env = unit(ref[start:start + size, :])
            env_hat[place:place + size, :] = env
            rows_k[:, place:place + size] = fourth(dot(points, env))
            place += size


def slice_kernel(descriptors, out):
    half = pl.multiple_of((lax.axis_index("sp") % 2) * 1024, 1024)
    out[...] = descriptors[pl.ds(half, 1024), :]


def split_kernel(near, *outs):
    size = near.shape[0] // len(outs)
    for i, out in enumerate(outs):
        out[...] = near[size * i:size * i + size, :]


def own_kernel(own_env, own_points, sib_points, env_hat, rows_k, gram, points_hat):
    points_hat[:256, :] = unit(own_points[...])
    points_hat[256:, :] = unit(sib_points[...])
    rows_of(points_hat[...], (own_env,), env_hat, rows_k)
    gram[...] = dot(rows_k[...], rows_k[:256, :])


def kernel_values(point_hat, envs, kept):
    place = 0
    for env in envs:
        for start in range(0, env.shape[0], CHUNK):
            kept[:, place:place + CHUNK] = fourth(dot(point_hat, env[start:start + CHUNK, :]))
            place += CHUNK


def products(rows, kept):
    total, place = None, 0
    for row in rows:
        term = dot(row[...], kept[:, place:place + row.shape[1]])
        total = term if total is None else total + term
        place += row.shape[1]
    return total


def give(gram, own_out, sib_out, t=slice(None)):
    total = (gram * weight_row()).astype(BF16)
    own_out[t] = total[:256]
    sib_out[t] = total[256:]


def begin_kernel(points, env_a, rows_a, point_hat, gram, kept):
    point_hat[...] = unit(points[...])
    kernel_values(point_hat[...], (env_a,), kept)
    gram[...] = products((rows_a,), kept)


def more_kernel(*refs):
    points_hat, gram, first_hat, first_gram, second_hat, second_gram, third, env_a, rows_a = refs[2 * PIECES:-5]
    env_hat, rows_k, own, sib, kept = refs[-5:]
    half = env_hat.shape[0]
    rows_of(points_hat[...], refs[:2 * PIECES], env_hat, rows_k)
    give(gram[...] + dot(rows_k[...], rows_k[:256, :]), own, sib, 0)
    for t, (point_hat, begun) in enumerate(((first_hat, first_gram), (second_hat, second_gram))):
        kernel_values(point_hat[...], (env_hat,), kept)
        give(begun[...] + products((rows_k,), kept), own, sib, 1 + t)
    kernel_values(unit(third[...]), (env_a, env_hat), kept)
    give(products((rows_a, rows_k), kept), own, sib, 3)


def column_kernel(points, *refs):
    kernel_values(unit(points[...]), refs[:2], refs[6])
    give(products(refs[2:4], refs[6]), refs[4], refs[5])


def pack_kernel(own, own_last, swapped, swapped_last, out):
    even_x = lax.axis_index("env") % 2 == 0
    shift = jnp.logical_and(even_x, lax.axis_index("sp") % 2 == 0)
    for e in range(8):
        rows = slice(32 * e, 32 * e + 32)
        for m in range(4):
            out[e, m] = own[m, rows, :]
        out[e, 4] = own_last[rows, :]
        for m in range(1, 4):
            out[e, 4 + m] = jnp.where(shift, swapped[m - 1, rows, :], swapped[m, rows, :])
        out[e, 8] = jnp.where(shift, swapped[3, rows, :], swapped_last[rows, :])


def finish_kernel(pieces, out):
    core = lax.axis_index("sp") % 2

    def total(parity, slot):
        value = None
        for e in range(parity, 8, 2):
            term = pieces[e, slot].astype(F32) * source_weight(e)
            value = term if value is None else value + term
        return value

    out[0] = total(0, 0)
    for m in range(1, 5):
        out[4 * m] = total(0, m)
        out[4 * m - 2] = total(1, m)
        out[4 * m - 3 + 2 * core] = total(0, 4 + m)
        out[4 * m - 1 - 2 * core] = total(1, 4 + m)


def vmem_spec():
    return pl.BlockSpec(memory_space=pltpu.VMEM)


def shape(*dims, dtype=BF16):
    return jax.ShapeDtypeStruct(dims, dtype)


def call(body, out_shape, n_in, flops, bytes_accessed, scratch=()):
    many = isinstance(out_shape, (tuple, list))
    return pl.pallas_call(
        body,
        out_shape=out_shape,
        in_specs=[vmem_spec() for _ in range(n_in)],
        out_specs=[vmem_spec() for _ in out_shape] if many else vmem_spec(),
        scratch_shapes=scratch,
        compiler_params=pltpu.CompilerParams(vmem_limit_bytes=VMEM_LIMIT),
        cost_estimate=pl.CostEstimate(flops=flops, bytes_accessed=bytes_accessed, transcendentals=0),
    )


def on_device(descriptors, sparse_points):
    barrier = lax.optimization_barrier

    def rows(body, envs, sums, n_in, *args):
        return call(body, (shape(envs, 512), shape(512, envs)) + sums, n_in, envs * 786432, envs << 12)(*args)

    gram_shape = shape(512, 256, dtype=F32)
    pair = (shape(256, 256), shape(256, 256))

    column = fetch(sparse_points, first_column)
    sib_points = fetch(sparse_points, other_core)
    env_a, rows_a, gram, points_hat = rows(
        own_kernel, 2048, (gram_shape, shape(512, 512)), 3, descriptors, sparse_points, sib_points
    )
    columns = [column]
    column, later, env_a, rows_a, gram, points_hat = barrier(
        (column, descriptors, env_a, rows_a, gram, points_hat)
    )

    kept = (pltpu.VMEM((256, 2048), BF16),)

    def begin(points):
        return call(begin_kernel, (shape(256, 512), gram_shape), 3, 1 << 30, 1 << 22, kept)(points, env_a, rows_a)

    columns.append(fetch(column, next_z))
    near = fetch(call(slice_kernel, shape(1024, 512), 1, 0, 1 << 21)(later), near_x)
    column, *begun = barrier((columns[1], *begin(columns[0])))

    columns.append(fetch(column, next_z))
    near, *others = barrier((near, *begin(column)))
    begun += others
    near = call(split_kernel, PIECES * (shape(1024 // PIECES, 512),), 1, 0, 1 << 21)(near)
    far = [fetch(piece, other_core) for piece in near]

    last = fetch(columns[2], next_z)
    four = (shape(4, 256, 256), shape(4, 256, 256))
    env_b, rows_b, own, sib = call(
        more_kernel, (shape(2048, 512), shape(512, 2048)) + four, 2 * PIECES + 9, 11 << 29, 1 << 24,
        (pltpu.VMEM((256, 4096), BF16),)
    )(*near, *far, points_hat, gram, *begun, columns[2], env_a, rows_a)
    swapped = fetch(sib, other_core)
    last, own = barrier((last, own))

    own_last, sib_last = call(
        column_kernel, pair, 5, 2 * 1073741824, 1 << 23, (pltpu.VMEM((256, 4096), BF16),)
    )(last, env_a, env_b, rows_a, rows_b)
    packed = call(pack_kernel, shape(8, 9, 32, 256), 4, 0, 1 << 21)(
        own, own_last, swapped, fetch(sib_last, other_core)
    )
    pieces = lax.all_to_all(packed, "env", 0, 0, tiled=True)
    return call(finish_kernel, shape(17, 32, 256, dtype=F32), 1, 0, 1 << 21)(pieces)[None]


def solution(mesh):
    placed = (P("env", None), P("sp", None))
    return jax.shard_map(
        on_device, mesh=mesh, in_specs=placed, out_specs=P("sp", None, "env", None), check_vma=False
    )
```

```python
import functools

import jax
import jax.numpy as jnp
from jax import lax
from jax.experimental import pallas as pl
from jax.experimental.pallas import tpu as pltpu
from jax.sharding import PartitionSpec as P


F32, BF16 = jnp.float32, jnp.bfloat16
NT = (((1,), (1,)), ((), ()))
VMEM_LIMIT = 20 * 1024 * 1024


def split_index(i):
    env, sp = divmod(i, 32)
    y_hi, x = divmod(env, 4)
    q, core = divmod(sp, 2)
    z, y_lo = divmod(q, 2)
    return y_hi, x, z, y_lo, core


def join_index(y_hi, x, z, y_lo, core):
    return ((y_hi % 2) * 4 + x % 4) * 32 + ((z % 8) * 2 + y_lo % 2) * 2 + core % 2


def fetch(value, source_of):
    pairs = [(join_index(*source_of(*split_index(i))), i) for i in range(256)]
    return lax.ppermute(value, ("env", "sp"), pairs)


def other_core(y_hi, x, z, y_lo, core):
    return y_hi, x, z, y_lo, 1 - core


def near_x(y_hi, x, z, y_lo, core):
    return y_hi, x + 1 - 2 * core, z, y_lo, core


def next_z(y_hi, x, z, y_lo, core):
    return y_hi, x, z + 1, y_lo, core


def first_column(y_hi, x, z, y_lo, core):
    if x % 2 == 0:
        return y_hi, x, z + 1, y_lo, core
    y = (y_hi * 2 + y_lo + 1 - 2 * core) % 4
    return y // 2, x, z + y_lo, y % 2, core


def unit(values):
    values = values.astype(F32)
    total = jnp.sum(values * values, axis=1, keepdims=True)
    return (values * lax.rsqrt(total + 1e-06)).astype(BF16)


def fourth(products):
    squares = products * products
    return (squares * squares).astype(BF16)


def dot(a, b):
    return lax.dot_general(a, b, NT, preferred_element_type=F32)


CHUNK = 512
PIECES = 4


def weight_row():
    env = lax.axis_index("env")
    group = (env // 4) * 2 + (env % 4) // 2
    lanes = lax.broadcasted_iota(jnp.int32, (1, 256), 1)
    return (1.0 + ((lanes + 64 * group) % 256).astype(F32) / 256.0) * (16.0 / 16384.0)


def source_weight(e):
    group = (e // 4) * 2 + (e % 4) // 2
    lanes = lax.broadcasted_iota(jnp.int32, (1, 256), 1)
    return 1.0 / (1.0 + ((lanes + 64 * group) % 256).astype(F32) / 256.0)


def rows_of(points, raw, env_hat, rows_k):
    place = 0
    for ref in raw:
        for start in range(0, ref.shape[0], CHUNK):
            size = min(CHUNK, ref.shape[0] - start)
            env = unit(ref[start:start + size, :])
            env_hat[place:place + size, :] = env
            rows_k[:, place:place + size] = fourth(dot(points, env))
            place += size


def slice_kernel(descriptors, out, sem):
    half = pl.multiple_of((lax.axis_index("sp") % 2) * 1024, 1024)
    copy = pltpu.make_async_copy(descriptors.at[pl.ds(half, 1024), :], out, sem)
    copy.start()
    copy.wait()


def split_kernel(near, *outs):
    size = near.shape[0] // len(outs)
    for i, out in enumerate(outs):
        out[...] = near[size * i:size * i + size, :]


def own_kernel(own_env, own_points, sib_points, env_hat, rows_k, gram, points_hat):
    points_hat[:256, :] = unit(own_points[...])
    points_hat[256:, :] = unit(sib_points[...])
    rows_of(points_hat[...], (own_env,), env_hat, rows_k)
    gram[...] = dot(rows_k[...], rows_k[:256, :])


def kernel_values(point_hat, envs, kept):
    place = 0
    for env in envs:
        for start in range(0, env.shape[0], CHUNK):
            kept[:, place:place + CHUNK] = fourth(dot(point_hat, env[start:start + CHUNK, :]))
            place += CHUNK


def products(rows, kept):
    total, place = None, 0
    for row in rows:
        term = dot(row[...], kept[:, place:place + row.shape[1]])
        total = term if total is None else total + term
        place += row.shape[1]
    return total


def give(gram, own_out, sib_out):
    total = (gram * weight_row()).astype(BF16)
    own_out[...] = total[:256]
    sib_out[...] = total[256:]


def more_kernel(*refs):
    points_hat, gram, env_hat, rows_k, own_out, sib_out = refs[2 * PIECES:]
    rows_of(points_hat[...], refs[:2 * PIECES], env_hat, rows_k)
    give(gram[...] + dot(rows_k[...], rows_k[:256, :]), own_out, sib_out)


def column_kernel(points, *refs):
    kernel_values(unit(points[...]), refs[:2], refs[6])
    give(products(refs[2:4], refs[6]), refs[4], refs[5])


def pack_kernel(*refs):
    own, swapped, out = refs[:5], refs[5:10], refs[10]
    even_x = lax.axis_index("env") % 2 == 0
    shift = jnp.logical_and(even_x, lax.axis_index("sp") % 2 == 0)
    for e in range(8):
        rows = slice(32 * e, 32 * e + 32)
        for m in range(5):
            out[e, m] = own[m][rows, :]
        for m in range(1, 5):
            out[e, 4 + m] = jnp.where(shift, swapped[m - 1][rows, :], swapped[m][rows, :])


def finish_kernel(pieces, out):
    core = lax.axis_index("sp") % 2

    def total(parity, slot):
        value = None
        for e in range(parity, 8, 2):
            term = pieces[e, slot].astype(F32) * source_weight(e)
            value = term if value is None else value + term
        return value

    out[0] = total(0, 0)
    for m in range(1, 5):
        out[4 * m] = total(0, m)
        out[4 * m - 2] = total(1, m)
        out[4 * m - 3 + 2 * core] = total(0, 4 + m)
        out[4 * m - 1 - 2 * core] = total(1, 4 + m)


def vmem_spec():
    return pl.BlockSpec(memory_space=pltpu.VMEM)


def shape(*dims, dtype=BF16):
    return jax.ShapeDtypeStruct(dims, dtype)


def call(body, out_shape, n_in, flops, bytes_accessed, scratch=()):
    many = isinstance(out_shape, (tuple, list))
    return pl.pallas_call(
        body,
        out_shape=out_shape,
        in_specs=[vmem_spec() for _ in range(n_in)],
        out_specs=[vmem_spec() for _ in out_shape] if many else vmem_spec(),
        scratch_shapes=scratch,
        compiler_params=pltpu.CompilerParams(vmem_limit_bytes=VMEM_LIMIT),
        cost_estimate=pl.CostEstimate(flops=flops, bytes_accessed=bytes_accessed, transcendentals=0),
    )


def on_device(descriptors, sparse_points):
    barrier = lax.optimization_barrier

    def rows(body, envs, sums, n_in, *args):
        return call(body, (shape(envs, 512), shape(512, envs)) + sums, n_in, envs * 786432, envs << 12)(*args)

    gram_shape = shape(512, 256, dtype=F32)
    pair = (shape(256, 256), shape(256, 256))

    columns = [fetch(sparse_points, first_column)]
    sib_points = fetch(sparse_points, other_core)
    near = pl.pallas_call(
        slice_kernel,
        out_shape=shape(1024, 512),
        in_specs=[pl.BlockSpec(memory_space=pl.ANY)],
        out_specs=vmem_spec(),
        scratch_shapes=(pltpu.SemaphoreType.DMA,),
        compiler_params=pltpu.CompilerParams(vmem_limit_bytes=61 * 1024 * 1024),
        cost_estimate=pl.CostEstimate(flops=0, bytes_accessed=1 << 21, transcendentals=0),
    )(descriptors)
    near = fetch(near, near_x)
    env_a, rows_a, gram, points_hat = rows(
        own_kernel, 2048, (gram_shape, shape(512, 512)), 3, descriptors, sparse_points, sib_points
    )
    column, env_a, rows_a, gram, points_hat = barrier((columns[0], env_a, rows_a, gram, points_hat))
    near, _ = barrier((near, column))

    columns.append(fetch(column, next_z))
    near = call(split_kernel, PIECES * (shape(1024 // PIECES, 512),), 1, 0, 1 << 21)(near)
    far = [fetch(piece, other_core) for piece in near]
    env_b, rows_b, *sums = rows(more_kernel, 2048, pair, 2 * PIECES + 2, *near, *far, points_hat, gram)

    def take(points):
        return call(
            column_kernel, pair, 5, 2 * 1073741824, 1 << 23, (pltpu.VMEM((256, 4096), BF16),)
        )(points, env_a, env_b, rows_a, rows_b)

    columns.append(fetch(columns[1], next_z))
    sums += take(columns[0]) + take(columns[1])
    column, *sums = barrier((columns[2], *sums))

    last = fetch(column, next_z)
    sums += take(column)
    owns, swapped = sums[0::2], [fetch(sib, other_core) for sib in sums[1::2]]
    last, *sums = barrier((last, *owns, *swapped))
    owns, swapped = sums[:4], sums[4:]

    own, sib = take(last)
    packed = call(pack_kernel, shape(8, 9, 32, 256), 10, 0, 1 << 21)(*owns, own, *swapped, fetch(sib, other_core))
    pieces = lax.all_to_all(packed, "env", 0, 0, tiled=True)
    return call(finish_kernel, shape(17, 32, 256, dtype=F32), 1, 0, 1 << 21)(pieces)[None]


def solution(mesh):
    placed = (P("env", None), P("sp", None))
    return jax.shard_map(
        on_device, mesh=mesh, in_specs=placed, out_specs=P("sp", None, "env", None), check_vma=False
    )
```

```python
import functools

import jax
import jax.numpy as jnp
from jax import lax
from jax.experimental import pallas as pl
from jax.experimental.pallas import tpu as pltpu
from jax.sharding import PartitionSpec as P


F32, BF16 = jnp.float32, jnp.bfloat16
NT = (((1,), (1,)), ((), ()))
VMEM_LIMIT = 20 * 1024 * 1024


def split_index(i):
    env, sp = divmod(i, 32)
    y_hi, x = divmod(env, 4)
    q, core = divmod(sp, 2)
    z, y_lo = divmod(q, 2)
    return y_hi, x, z, y_lo, core


def join_index(y_hi, x, z, y_lo, core):
    return ((y_hi % 2) * 4 + x % 4) * 32 + ((z % 8) * 2 + y_lo % 2) * 2 + core % 2


def fetch(value, source_of):
    pairs = [(join_index(*source_of(*split_index(i))), i) for i in range(256)]
    return lax.ppermute(value, ("env", "sp"), pairs)


def other_core(y_hi, x, z, y_lo, core):
    return y_hi, x, z, y_lo, 1 - core


def near_x(y_hi, x, z, y_lo, core):
    return y_hi, x + 1 - 2 * core, z, y_lo, core


def next_z(y_hi, x, z, y_lo, core):
    return y_hi, x, z + 1, y_lo, core


def first_column(y_hi, x, z, y_lo, core):
    if x % 2 == 0:
        return y_hi, x, z + 1, y_lo, core
    y = (y_hi * 2 + y_lo + 1 - 2 * core) % 4
    return y // 2, x, z + y_lo, y % 2, core


def unit(values):
    values = values.astype(F32)
    total = jnp.sum(values * values, axis=1, keepdims=True)
    return (values * lax.rsqrt(total + 1e-06)).astype(BF16)


def fourth(products):
    squares = products * products
    return (squares * squares).astype(BF16)


def dot(a, b):
    return lax.dot_general(a, b, NT, preferred_element_type=F32)


CHUNK = 512
PIECES = 4


def weight_row():
    env = lax.axis_index("env")
    group = (env // 4) * 2 + (env % 4) // 2
    lanes = lax.broadcasted_iota(jnp.int32, (1, 256), 1)
    return (1.0 + ((lanes + 64 * group) % 256).astype(F32) / 256.0) * (16.0 / 16384.0)


def source_weight(e):
    group = (e // 4) * 2 + (e % 4) // 2
    lanes = lax.broadcasted_iota(jnp.int32, (1, 256), 1)
    return 1.0 / (1.0 + ((lanes + 64 * group) % 256).astype(F32) / 256.0)


def rows_of(points, raw, env_hat, rows_k):
    place = 0
    for ref in raw:
        for start in range(0, ref.shape[0], CHUNK):
            size = min(CHUNK, ref.shape[0] - start)
            env = unit(ref[start:start + size, :])
            env_hat[place:place + size, :] = env
            rows_k[:, place:place + size] = fourth(dot(points, env))
            place += size


def slice_kernel(descriptors, out, sems):
    half = pl.multiple_of((lax.axis_index("sp") % 2) * 1024, 1024)
    copies = []
    for i in range(4):
        rows = descriptors.at[pl.ds(half + 256 * i, 256), :]
        copies.append(pltpu.make_async_copy(rows, out.at[pl.ds(256 * i, 256), :], sems.at[i]))
        copies[i].start()
    for copy in copies:
        copy.wait()


def split_kernel(near, *outs):
    size = near.shape[0] // len(outs)
    for i, out in enumerate(outs):
        out[...] = near[size * i:size * i + size, :]


def own_kernel(own_env, own_points, sib_points, env_hat, rows_k, gram, points_hat):
    points_hat[:256, :] = unit(own_points[...])
    points_hat[256:, :] = unit(sib_points[...])
    rows_of(points_hat[...], (own_env,), env_hat, rows_k)
    gram[...] = dot(rows_k[...], rows_k[:256, :])


def kernel_values(point_hat, envs, kept):
    place = 0
    for env in envs:
        for start in range(0, env.shape[0], CHUNK):
            kept[:, place:place + CHUNK] = fourth(dot(point_hat, env[start:start + CHUNK, :]))
            place += CHUNK


def products(rows, kept):
    total, place = None, 0
    for row in rows:
        term = dot(row[...], kept[:, place:place + row.shape[1]])
        total = term if total is None else total + term
        place += row.shape[1]
    return total


def give(gram, own_out, sib_out):
    total = (gram * weight_row()).astype(BF16)
    own_out[...] = total[:256]
    sib_out[...] = total[256:]


def more_kernel(*refs):
    points_hat, gram, env_hat, rows_k, own_out, sib_out = refs[2 * PIECES:]
    rows_of(points_hat[...], refs[:2 * PIECES], env_hat, rows_k)
    give(gram[...] + dot(rows_k[...], rows_k[:256, :]), own_out, sib_out)


def column_kernel(points, *refs):
    kernel_values(unit(points[...]), refs[:2], refs[6])
    give(products(refs[2:4], refs[6]), refs[4], refs[5])


def pack_kernel(*refs):
    own, swapped, out = refs[:5], refs[5:10], refs[10]
    even_x = lax.axis_index("env") % 2 == 0
    shift = jnp.logical_and(even_x, lax.axis_index("sp") % 2 == 0)
    for e in range(8):
        rows = slice(32 * e, 32 * e + 32)
        for m in range(5):
            out[e, m] = own[m][rows, :]
        for m in range(1, 5):
            out[e, 4 + m] = jnp.where(shift, swapped[m - 1][rows, :], swapped[m][rows, :])


def finish_kernel(pieces, out):
    core = lax.axis_index("sp") % 2

    def total(parity, slot):
        value = None
        for e in range(parity, 8, 2):
            term = pieces[e, slot].astype(F32) * source_weight(e)
            value = term if value is None else value + term
        return value

    out[0] = total(0, 0)
    for m in range(1, 5):
        out[4 * m] = total(0, m)
        out[4 * m - 2] = total(1, m)
        out[4 * m - 3 + 2 * core] = total(0, 4 + m)
        out[4 * m - 1 - 2 * core] = total(1, 4 + m)


def vmem_spec():
    return pl.BlockSpec(memory_space=pltpu.VMEM)


def shape(*dims, dtype=BF16):
    return jax.ShapeDtypeStruct(dims, dtype)


def call(body, out_shape, n_in, flops, bytes_accessed, scratch=()):
    many = isinstance(out_shape, (tuple, list))
    return pl.pallas_call(
        body,
        out_shape=out_shape,
        in_specs=[vmem_spec() for _ in range(n_in)],
        out_specs=[vmem_spec() for _ in out_shape] if many else vmem_spec(),
        scratch_shapes=scratch,
        compiler_params=pltpu.CompilerParams(vmem_limit_bytes=VMEM_LIMIT),
        cost_estimate=pl.CostEstimate(flops=flops, bytes_accessed=bytes_accessed, transcendentals=0),
    )


def on_device(descriptors, sparse_points):
    barrier = lax.optimization_barrier

    def rows(body, envs, sums, n_in, *args):
        return call(body, (shape(envs, 512), shape(512, envs)) + sums, n_in, envs * 786432, envs << 12)(*args)

    gram_shape = shape(512, 256, dtype=F32)
    pair = (shape(256, 256), shape(256, 256))

    columns = [fetch(sparse_points, first_column)]
    sib_points = fetch(sparse_points, other_core)
    near = pl.pallas_call(
        slice_kernel,
        out_shape=shape(1024, 512),
        in_specs=[pl.BlockSpec(memory_space=pl.ANY)],
        out_specs=pl.BlockSpec(memory_space=pl.ANY),
        scratch_shapes=(pltpu.SemaphoreType.DMA((4,)),),
        compiler_params=pltpu.CompilerParams(vmem_limit_bytes=61 * 1024 * 1024),
        cost_estimate=pl.CostEstimate(flops=0, bytes_accessed=1 << 21, transcendentals=0),
    )(descriptors)
    near = fetch(near, near_x)
    env_a, rows_a, gram, points_hat = rows(
        own_kernel, 2048, (gram_shape, shape(512, 512)), 3, descriptors, sparse_points, sib_points
    )
    column, env_a, rows_a, gram, points_hat = barrier((columns[0], env_a, rows_a, gram, points_hat))
    near, _ = barrier((near, column))

    columns.append(fetch(column, next_z))
    near = call(split_kernel, PIECES * (shape(1024 // PIECES, 512),), 1, 0, 1 << 21)(near)
    far = [fetch(piece, other_core) for piece in near]
    env_b, rows_b, *sums = rows(more_kernel, 2048, pair, 2 * PIECES + 2, *near, *far, points_hat, gram)

    def take(points):
        return call(
            column_kernel, pair, 5, 2 * 1073741824, 1 << 23, (pltpu.VMEM((256, 4096), BF16),)
        )(points, env_a, env_b, rows_a, rows_b)

    columns.append(fetch(columns[1], next_z))
    sums += take(columns[0]) + take(columns[1])
    column, *sums = barrier((columns[2], *sums))

    last = fetch(column, next_z)
    sums += take(column)
    owns, swapped = sums[0::2], [fetch(sib, other_core) for sib in sums[1::2]]
    last, *sums = barrier((last, *owns, *swapped))
    owns, swapped = sums[:4], sums[4:]

    own, sib = take(last)
    packed = call(pack_kernel, shape(8, 9, 32, 256), 10, 0, 1 << 21)(*owns, own, *swapped, fetch(sib, other_core))
    pieces = lax.all_to_all(packed, "env", 0, 0, tiled=True)
    return call(finish_kernel, shape(17, 32, 256, dtype=F32), 1, 0, 1 << 21)(pieces)[None]


def solution(mesh):
    placed = (P("env", None), P("sp", None))
    return jax.shard_map(
        on_device, mesh=mesh, in_specs=placed, out_specs=P("sp", None, "env", None), check_vma=False
    )
```

```python
import functools

import jax
import jax.numpy as jnp
from jax import lax
from jax.experimental import pallas as pl
from jax.experimental.pallas import tpu as pltpu
from jax.sharding import PartitionSpec as P


F32, BF16 = jnp.float32, jnp.bfloat16
NT = (((1,), (1,)), ((), ()))
VMEM_LIMIT = 20 * 1024 * 1024


def split_index(i):
    env, sp = divmod(i, 32)
    y_hi, x = divmod(env, 4)
    q, core = divmod(sp, 2)
    z, y_lo = divmod(q, 2)
    return y_hi, x, z, y_lo, core


def join_index(y_hi, x, z, y_lo, core):
    return ((y_hi % 2) * 4 + x % 4) * 32 + ((z % 8) * 2 + y_lo % 2) * 2 + core % 2


def fetch(value, source_of):
    pairs = [(join_index(*source_of(*split_index(i))), i) for i in range(256)]
    return lax.ppermute(value, ("env", "sp"), pairs)


def other_core(y_hi, x, z, y_lo, core):
    return y_hi, x, z, y_lo, 1 - core


def near_x(y_hi, x, z, y_lo, core):
    return y_hi, x + 1 - 2 * core, z, y_lo, core


def next_z(y_hi, x, z, y_lo, core):
    return y_hi, x, z + 1, y_lo, core


def first_column(y_hi, x, z, y_lo, core):
    if x % 2 == 0:
        return y_hi, x, z + 1, y_lo, core
    y = (y_hi * 2 + y_lo + 1 - 2 * core) % 4
    return y // 2, x, z + y_lo, y % 2, core


def unit(values):
    values = values.astype(F32)
    total = jnp.sum(values * values, axis=1, keepdims=True)
    return (values * lax.rsqrt(total + 1e-06)).astype(BF16)


def fourth(products):
    squares = products * products
    return (squares * squares).astype(BF16)


def dot(a, b):
    return lax.dot_general(a, b, NT, preferred_element_type=F32)


CHUNK = 512
PIECES = 4


def weight_row():
    env = lax.axis_index("env")
    group = (env // 4) * 2 + (env % 4) // 2
    lanes = lax.broadcasted_iota(jnp.int32, (1, 256), 1)
    return (1.0 + ((lanes + 64 * group) % 256).astype(F32) / 256.0) * (16.0 / 16384.0)


def source_weight(e):
    group = (e // 4) * 2 + (e % 4) // 2
    lanes = lax.broadcasted_iota(jnp.int32, (1, 256), 1)
    return 1.0 / (1.0 + ((lanes + 64 * group) % 256).astype(F32) / 256.0)


def rows_of(points, raw, env_hat, rows_k):
    place = 0
    for ref in raw:
        for start in range(0, ref.shape[0], CHUNK):
            size = min(CHUNK, ref.shape[0] - start)
            env = unit(ref[start:start + size, :])
            env_hat[place:place + size, :] = env
            rows_k[:, place:place + size] = fourth(dot(points, env))
            place += size


def slice_kernel(descriptors, out, held, arrived, left):
    half = pl.multiple_of((lax.axis_index("sp") % 2) * 1024, 1024)
    inward, outward = [], []
    for i in range(4):
        part = pl.ds(256 * i, 256)
        source = descriptors.at[pl.ds(half + 256 * i, 256), :]
        inward.append(pltpu.make_async_copy(source, held.at[part, :], arrived.at[i]))
        outward.append(pltpu.make_async_copy(held.at[part, :], out.at[part, :], left.at[i]))
        inward[i].start()
    for i in range(4):
        inward[i].wait()
        outward[i].start()
    for copy in outward:
        copy.wait()


def split_kernel(near, *outs):
    size = near.shape[0] // len(outs)
    for i, out in enumerate(outs):
        out[...] = near[size * i:size * i + size, :]


def own_kernel(own_env, own_points, sib_points, env_hat, rows_k, gram, points_hat):
    points_hat[:256, :] = unit(own_points[...])
    points_hat[256:, :] = unit(sib_points[...])
    rows_of(points_hat[...], (own_env,), env_hat, rows_k)
    gram[...] = dot(rows_k[...], rows_k[:256, :])


def kernel_values(point_hat, envs, kept):
    place = 0
    for env in envs:
        for start in range(0, env.shape[0], CHUNK):
            kept[:, place:place + CHUNK] = fourth(dot(point_hat, env[start:start + CHUNK, :]))
            place += CHUNK


def products(rows, kept):
    total, place = None, 0
    for row in rows:
        term = dot(row[...], kept[:, place:place + row.shape[1]])
        total = term if total is None else total + term
        place += row.shape[1]
    return total


def give(gram, own_out, sib_out):
    total = (gram * weight_row()).astype(BF16)
    own_out[...] = total[:256]
    sib_out[...] = total[256:]


def more_kernel(*refs):
    points_hat, gram, env_hat, rows_k, own_out, sib_out = refs[2 * PIECES:]
    rows_of(points_hat[...], refs[:2 * PIECES], env_hat, rows_k)
    give(gram[...] + dot(rows_k[...], rows_k[:256, :]), own_out, sib_out)


def column_kernel(points, *refs):
    kernel_values(unit(points[...]), refs[:2], refs[6])
    give(products(refs[2:4], refs[6]), refs[4], refs[5])


def pack_kernel(*refs):
    own, swapped, out = refs[:5], refs[5:10], refs[10]
    even_x = lax.axis_index("env") % 2 == 0
    shift = jnp.logical_and(even_x, lax.axis_index("sp") % 2 == 0)
    for e in range(8):
        rows = slice(32 * e, 32 * e + 32)
        for m in range(5):
            out[e, m] = own[m][rows, :]
        for m in range(1, 5):
            out[e, 4 + m] = jnp.where(shift, swapped[m - 1][rows, :], swapped[m][rows, :])


def finish_kernel(pieces, out):
    core = lax.axis_index("sp") % 2

    def total(parity, slot):
        value = None
        for e in range(parity, 8, 2):
            term = pieces[e, slot].astype(F32) * source_weight(e)
            value = term if value is None else value + term
        return value

    out[0] = total(0, 0)
    for m in range(1, 5):
        out[4 * m] = total(0, m)
        out[4 * m - 2] = total(1, m)
        out[4 * m - 3 + 2 * core] = total(0, 4 + m)
        out[4 * m - 1 - 2 * core] = total(1, 4 + m)


def vmem_spec():
    return pl.BlockSpec(memory_space=pltpu.VMEM)


def shape(*dims, dtype=BF16):
    return jax.ShapeDtypeStruct(dims, dtype)


def call(body, out_shape, n_in, flops, bytes_accessed, scratch=()):
    many = isinstance(out_shape, (tuple, list))
    return pl.pallas_call(
        body,
        out_shape=out_shape,
        in_specs=[vmem_spec() for _ in range(n_in)],
        out_specs=[vmem_spec() for _ in out_shape] if many else vmem_spec(),
        scratch_shapes=scratch,
        compiler_params=pltpu.CompilerParams(vmem_limit_bytes=VMEM_LIMIT),
        cost_estimate=pl.CostEstimate(flops=flops, bytes_accessed=bytes_accessed, transcendentals=0),
    )


def on_device(descriptors, sparse_points):
    barrier = lax.optimization_barrier

    def rows(body, envs, sums, n_in, *args):
        return call(body, (shape(envs, 512), shape(512, envs)) + sums, n_in, envs * 786432, envs << 12)(*args)

    gram_shape = shape(512, 256, dtype=F32)
    pair = (shape(256, 256), shape(256, 256))

    columns = [fetch(sparse_points, first_column)]
    sib_points = fetch(sparse_points, other_core)
    near = pl.pallas_call(
        slice_kernel,
        out_shape=shape(1024, 512),
        in_specs=[pl.BlockSpec(memory_space=pl.ANY)],
        out_specs=pl.BlockSpec(memory_space=pl.ANY),
        scratch_shapes=(
            pltpu.VMEM((1024, 512), BF16),
            pltpu.SemaphoreType.DMA((4,)),
            pltpu.SemaphoreType.DMA((4,)),
        ),
        compiler_params=pltpu.CompilerParams(vmem_limit_bytes=61 * 1024 * 1024),
        cost_estimate=pl.CostEstimate(flops=0, bytes_accessed=1 << 21, transcendentals=0),
    )(descriptors)
    near = fetch(near, near_x)
    env_a, rows_a, gram, points_hat = rows(
        own_kernel, 2048, (gram_shape, shape(512, 512)), 3, descriptors, sparse_points, sib_points
    )
    column, env_a, rows_a, gram, points_hat = barrier((columns[0], env_a, rows_a, gram, points_hat))
    near, _ = barrier((near, column))

    columns.append(fetch(column, next_z))
    near = call(split_kernel, PIECES * (shape(1024 // PIECES, 512),), 1, 0, 1 << 21)(near)
    far = [fetch(piece, other_core) for piece in near]
    env_b, rows_b, *sums = rows(more_kernel, 2048, pair, 2 * PIECES + 2, *near, *far, points_hat, gram)

    def take(points):
        return call(
            column_kernel, pair, 5, 2 * 1073741824, 1 << 23, (pltpu.VMEM((256, 4096), BF16),)
        )(points, env_a, env_b, rows_a, rows_b)

    columns.append(fetch(columns[1], next_z))
    sums += take(columns[0]) + take(columns[1])
    column, *sums = barrier((columns[2], *sums))

    last = fetch(column, next_z)
    sums += take(column)
    owns, swapped = sums[0::2], [fetch(sib, other_core) for sib in sums[1::2]]
    last, *sums = barrier((last, *owns, *swapped))
    owns, swapped = sums[:4], sums[4:]

    own, sib = take(last)
    packed = call(pack_kernel, shape(8, 9, 32, 256), 10, 0, 1 << 21)(*owns, own, *swapped, fetch(sib, other_core))
    pieces = lax.all_to_all(packed, "env", 0, 0, tiled=True)
    return call(finish_kernel, shape(17, 32, 256, dtype=F32), 1, 0, 1 << 21)(pieces)[None]


def solution(mesh):
    placed = (P("env", None), P("sp", None))
    return jax.shard_map(
        on_device, mesh=mesh, in_specs=placed, out_specs=P("sp", None, "env", None), check_vma=False
    )
```

```python
import functools

import jax
import jax.numpy as jnp
from jax import lax
from jax.experimental import pallas as pl
from jax.experimental.pallas import tpu as pltpu
from jax.sharding import PartitionSpec as P


F32, BF16 = jnp.float32, jnp.bfloat16
NT = (((1,), (1,)), ((), ()))
VMEM_LIMIT = 20 * 1024 * 1024


def split_index(i):
    env, sp = divmod(i, 32)
    y_hi, x = divmod(env, 4)
    q, core = divmod(sp, 2)
    z, y_lo = divmod(q, 2)
    return y_hi, x, z, y_lo, core


def join_index(y_hi, x, z, y_lo, core):
    return ((y_hi % 2) * 4 + x % 4) * 32 + ((z % 8) * 2 + y_lo % 2) * 2 + core % 2


def fetch(value, source_of):
    pairs = [(join_index(*source_of(*split_index(i))), i) for i in range(256)]
    return lax.ppermute(value, ("env", "sp"), pairs)


def other_core(y_hi, x, z, y_lo, core):
    return y_hi, x, z, y_lo, 1 - core


def near_x(y_hi, x, z, y_lo, core):
    return y_hi, x + 1 - 2 * core, z, y_lo, core


def next_z(y_hi, x, z, y_lo, core):
    return y_hi, x, z + 1, y_lo, core


def first_column(y_hi, x, z, y_lo, core):
    if x % 2 == 0:
        return y_hi, x, z + 1, y_lo, core
    y = (y_hi * 2 + y_lo + 1 - 2 * core) % 4
    return y // 2, x, z + y_lo, y % 2, core


def unit(values):
    values = values.astype(F32)
    total = jnp.sum(values * values, axis=1, keepdims=True)
    return (values * lax.rsqrt(total + 1e-06)).astype(BF16)


def fourth(products):
    squares = products * products
    return (squares * squares).astype(BF16)


def dot(a, b):
    return lax.dot_general(a, b, NT, preferred_element_type=F32)


CHUNK = 512
PIECES = 4


def weight_row():
    env = lax.axis_index("env")
    group = (env // 4) * 2 + (env % 4) // 2
    lanes = lax.broadcasted_iota(jnp.int32, (1, 256), 1)
    return (1.0 + ((lanes + 64 * group) % 256).astype(F32) / 256.0) * (16.0 / 16384.0)


def source_weight(e):
    group = (e // 4) * 2 + (e % 4) // 2
    lanes = lax.broadcasted_iota(jnp.int32, (1, 256), 1)
    return 1.0 / (1.0 + ((lanes + 64 * group) % 256).astype(F32) / 256.0)


def rows_of(points, raw, env_hat, rows_k):
    place = 0
    for ref in raw:
        for start in range(0, ref.shape[0], CHUNK):
            size = min(CHUNK, ref.shape[0] - start)
            env = unit(ref[start:start + size, :])
            env_hat[place:place + size, :] = env
            rows_k[:, place:place + size] = fourth(dot(points, env))
            place += size


def slice_kernel(descriptors, out, held, arrived, left):
    half = pl.multiple_of((lax.axis_index("sp") % 2) * 1024, 1024)
    inward, outward = [], []
    for i in range(4):
        part = pl.ds(256 * i, 256)
        source = descriptors.at[pl.ds(half + 256 * i, 256), :]
        inward.append(pltpu.make_async_copy(source, held.at[part, :], arrived.at[i]))
        outward.append(pltpu.make_async_copy(held.at[part, :], out.at[part, :], left.at[i]))
        inward[i].start()
    for i in range(4):
        inward[i].wait()
        outward[i].start()
    for copy in outward:
        copy.wait()


def split_kernel(near, *outs):
    size = near.shape[0] // len(outs)
    for i, out in enumerate(outs):
        out[...] = near[size * i:size * i + size, :]


def own_kernel(own_env, own_points, sib_points, env_hat, rows_k, gram, points_hat):
    points_hat[:256, :] = unit(own_points[...])
    points_hat[256:, :] = unit(sib_points[...])
    rows_of(points_hat[...], (own_env,), env_hat, rows_k)
    gram[...] = dot(rows_k[...], rows_k[:256, :])


def kernel_values(point_hat, envs, kept):
    place = 0
    for env in envs:
        for start in range(0, env.shape[0], CHUNK):
            kept[:, place:place + CHUNK] = fourth(dot(point_hat, env[start:start + CHUNK, :]))
            place += CHUNK


def products(rows, kept):
    total, place = None, 0
    for row in rows:
        term = dot(row[...], kept[:, place:place + row.shape[1]])
        total = term if total is None else total + term
        place += row.shape[1]
    return total


def give(gram, own_out, sib_out):
    total = (gram * weight_row()).astype(BF16)
    own_out[...] = total[:256]
    sib_out[...] = total[256:]


def more_kernel(*refs):
    points_hat, gram, env_hat, rows_k, own_out, sib_out = refs[2 * PIECES:]
    rows_of(points_hat[...], refs[:2 * PIECES], env_hat, rows_k)
    give(gram[...] + dot(rows_k[...], rows_k[:256, :]), own_out, sib_out)


def column_kernel(points, *refs):
    kernel_values(unit(points[...]), refs[:2], refs[6])
    give(products(refs[2:4], refs[6]), refs[4], refs[5])


def pack_kernel(*refs):
    own, swapped, out = refs[:5], refs[5:10], refs[10]
    even_x = lax.axis_index("env") % 2 == 0
    shift = jnp.logical_and(even_x, lax.axis_index("sp") % 2 == 0)
    for e in range(8):
        rows = slice(32 * e, 32 * e + 32)
        for m in range(5):
            out[e, m] = own[m][rows, :]
        for m in range(1, 5):
            out[e, 4 + m] = jnp.where(shift, swapped[m - 1][rows, :], swapped[m][rows, :])


def finish_kernel(pieces, out):
    core = lax.axis_index("sp") % 2

    def total(parity, slot):
        value = None
        for e in range(parity, 8, 2):
            term = pieces[e, slot].astype(F32) * source_weight(e)
            value = term if value is None else value + term
        return value

    out[0] = total(0, 0)
    for m in range(1, 5):
        out[4 * m] = total(0, m)
        out[4 * m - 2] = total(1, m)
        out[4 * m - 3 + 2 * core] = total(0, 4 + m)
        out[4 * m - 1 - 2 * core] = total(1, 4 + m)


def vmem_spec():
    return pl.BlockSpec(memory_space=pltpu.VMEM)


def shape(*dims, dtype=BF16):
    return jax.ShapeDtypeStruct(dims, dtype)


def call(body, out_shape, n_in, flops, bytes_accessed, scratch=()):
    many = isinstance(out_shape, (tuple, list))
    return pl.pallas_call(
        body,
        out_shape=out_shape,
        in_specs=[vmem_spec() for _ in range(n_in)],
        out_specs=[vmem_spec() for _ in out_shape] if many else vmem_spec(),
        scratch_shapes=scratch,
        compiler_params=pltpu.CompilerParams(vmem_limit_bytes=VMEM_LIMIT),
        cost_estimate=pl.CostEstimate(flops=flops, bytes_accessed=bytes_accessed, transcendentals=0),
    )


def on_device(descriptors, sparse_points):
    barrier = lax.optimization_barrier

    def rows(body, envs, sums, n_in, *args):
        return call(body, (shape(envs, 512), shape(512, envs)) + sums, n_in, envs * 786432, envs << 12)(*args)

    gram_shape = shape(512, 256, dtype=F32)
    pair = (shape(256, 256), shape(256, 256))

    columns = [fetch(sparse_points, first_column)]
    sib_points = fetch(sparse_points, other_core)
    near = pl.pallas_call(
        slice_kernel,
        out_shape=shape(1024, 512),
        in_specs=[pl.BlockSpec(memory_space=pl.ANY)],
        out_specs=pl.BlockSpec(memory_space=pl.ANY),
        scratch_shapes=(
            pltpu.VMEM((1024, 512), BF16),
            pltpu.SemaphoreType.DMA((4,)),
            pltpu.SemaphoreType.DMA((4,)),
        ),
        compiler_params=pltpu.CompilerParams(vmem_limit_bytes=62 * 1024 * 1024),
        cost_estimate=pl.CostEstimate(flops=0, bytes_accessed=1 << 21, transcendentals=0),
    )(descriptors)
    near = fetch(near, near_x)
    env_a, rows_a, gram, points_hat = rows(
        own_kernel, 2048, (gram_shape, shape(512, 512)), 3, descriptors, sparse_points, sib_points
    )
    column, env_a, rows_a, gram, points_hat = barrier((columns[0], env_a, rows_a, gram, points_hat))
    near, _ = barrier((near, column))

    columns.append(fetch(column, next_z))
    near = call(split_kernel, PIECES * (shape(1024 // PIECES, 512),), 1, 0, 1 << 21)(near)
    far = [fetch(piece, other_core) for piece in near]
    env_b, rows_b, *sums = rows(more_kernel, 2048, pair, 2 * PIECES + 2, *near, *far, points_hat, gram)

    def take(points):
        return call(
            column_kernel, pair, 5, 2 * 1073741824, 1 << 23, (pltpu.VMEM((256, 4096), BF16),)
        )(points, env_a, env_b, rows_a, rows_b)

    columns.append(fetch(columns[1], next_z))
    sums += take(columns[0]) + take(columns[1])
    column, *sums = barrier((columns[2], *sums))

    last = fetch(column, next_z)
    sums += take(column)
    owns, swapped = sums[0::2], [fetch(sib, other_core) for sib in sums[1::2]]
    last, *sums = barrier((last, *owns, *swapped))
    owns, swapped = sums[:4], sums[4:]

    own, sib = take(last)
    packed = call(pack_kernel, shape(8, 9, 32, 256), 10, 0, 1 << 21)(*owns, own, *swapped, fetch(sib, other_core))
    pieces = lax.all_to_all(packed, "env", 0, 0, tiled=True)
    return call(finish_kernel, shape(17, 32, 256, dtype=F32), 1, 0, 1 << 21)(pieces)[None]


def solution(mesh):
    placed = (P("env", None), P("sp", None))
    return jax.shard_map(
        on_device, mesh=mesh, in_specs=placed, out_specs=P("sp", None, "env", None), check_vma=False
    )
```
